32 devices in a mesh: ctx: 4 (over y, x), grp: 8 (over z, core).
Axes of the slice: x: 2, y: 2, z: 4, core: 2. Of those that a mesh axis runs over, the one named last changes fastest.
Arguments:
- q_in: bfloat16 [512, 8192], P('ctx', 'grp'), may hold values from -170 to 170
- k_in: bfloat16 [512, 8192], P('ctx', 'grp'), may hold values from -6 to 6
- v_in: bfloat16 [512, 8192], P('ctx', 'grp'), may hold values from -6 to 6
- fir: float32 [3, 3, 8192], P(None, None, 'grp'), may hold values from -3 to 3
- skip: float32 [8192], P('grp'), may hold values from 0.2 to 1
- taps: bfloat16 [64, 512], P('grp'), may hold values from -0.5 to 0.5
- segments: int32 [512], P('ctx'), may hold values from 0 to 1, never falling along the last dimension, each value on 1 to 384 neighbouring positions
- gain: float32 [8192], P('grp'), may hold values from 0.1 to 1.9
Outputs:
- mixed: bfloat16 [512, 8192], P('ctx', 'grp')
The draws below stay inside these ranges and needn't reach their ends.
All inputs are finite; a program needn't handle non-finite values.
Results may differ from the reference program's by a relative error of at most 0.0085.
Values may be sent and summed in bfloat16 or wider, within the bound.
A program may use at most 64 MiB of HBM per device.

```python
import math
import jax
import jax.numpy as jnp
import numpy as np
from jax import lax

D = 8192
GW = 128
TOK_DEV = 128
TOKENS = 512
FG = 64
SEGS = 2
LONGEST = 384


def draw_q_in(key, part):
    key_base = jax.random.fold_in(key, 11)
    key_cols = jax.random.fold_in(key, 12)
    key_rows = jax.random.fold_in(key, 13)
    base = jax.random.truncated_normal(key_base, -4.0, 4.0, (TOKENS, D), jnp.float32)
    rise = 3.0
    top = 4.0
    columns = jnp.exp(jax.random.uniform(key_cols, (D,), jnp.float32, 0.0, math.log(top)))
    columns = columns * rise ** (jnp.arange(D, dtype=jnp.float32) / D)
    rows_scale = jnp.exp(jax.random.uniform(key_rows, (TOKENS, 1), jnp.float32, 0.0, math.log(3.5)))
    return (base * rows_scale * columns).astype(jnp.bfloat16)


def block_scale(stream_key, dims, pieces, smallest, largest):
    def one(axis_at, blocks):
        draws = jax.random.uniform(jax.random.fold_in(jax.random.fold_in(stream_key, 6), axis_at), (blocks,), jnp.float32, smallest / len(pieces), largest / len(pieces))
        return jnp.repeat(jnp.exp(draws), dims[axis_at] // blocks).reshape((-1,) + (1,) * (len(dims) - axis_at - 1))

    level = one(*pieces[0])
    for cut in pieces[1:]:
        level = level * one(*cut)
    return level


def split_up(count, total, limit, slope):
    weights = [(1 << 20) // math.isqrt(grade ** slope) + 1 for grade in range(2, count + 1)]
    rest, counts = total - limit - (count - 1), [1] * (count - 1)
    while rest > 0:
        free = [i for i in range(count - 1) if counts[i] < limit]
        mass, left = sum([weights[i] for i in free]), rest
        for i in free:
            addition = min(limit - counts[i], max(1, left * weights[i] // mass), rest)
            counts[i] = counts[i] + addition
            rest = rest - addition
    return np.array([limit] + counts)


def uneven(stream_key, number_of, total, reach, skew):
    if number_of == 2:
        one = jax.random.randint(stream_key, (), max(1, total - reach), min(reach, total - 1) + 1)
        return jnp.stack([one, total - one])
    lengths = jnp.asarray(split_up(number_of, total, reach, skew), jnp.int32)
    pairs = (number_of - 1) // 2
    source_of, sink = lengths[1:1 + 2 * pairs:2], lengths[2:2 + 2 * pairs:2]
    room = jnp.minimum(source_of - 1, reach - sink)
    passed = jax.random.randint(jax.random.fold_in(stream_key, 1), (pairs,), 0, 1 << 20) % (room + 1)
    lengths = lengths.at[1:1 + 2 * pairs:2].set(source_of - passed).at[2:2 + 2 * pairs:2].set(sink + passed)
    return lengths[jax.random.permutation(jax.random.fold_in(stream_key, 2), number_of)]


def scatter_about(own_key, dims, deviation, limit, shards=(), kind=jnp.bfloat16):
    factor_of = block_scale(own_key, dims, shards, -0.22, 0.18) if shards else 1.0
    result = jax.random.normal(own_key, dims, jnp.float32) * deviation * factor_of
    return jnp.minimum(jnp.maximum(result, -limit), limit).astype(kind)


def setup_inputs(seed: int = 0) -> dict:
    keys = jax.random.split(jax.random.key(seed), 9)
    q_in = draw_q_in(jax.random.fold_in(keys[8], 71), 0)
    k_in = scatter_about(keys[1], (TOKENS, D), 1.0, 6.0, ((0, 4), (1, 8)))
    v_in = scatter_about(keys[2], (TOKENS, D), 1.0, 6.0, ((0, 4), (1, 8)))
    fir = scatter_about(keys[3], (3, 3, D), 0.6, 3.0, ((2, 8),), jnp.float32)
    skip = jnp.clip(jnp.exp(math.log(1.0) - 1.609438 * jax.random.uniform(keys[4], (D,), jnp.float32) ** block_scale(keys[4], (D,), ((0, 8),), -0.2, 0.2)), 0.2, 1.0)
    taps = scatter_about(keys[5], (FG, TOKENS), (TOKENS // 4) ** -0.5, 0.5, ((0, 8),))
    segments = jnp.searchsorted(jnp.cumsum(uneven(keys[6], SEGS, TOKENS, LONGEST, 2)), jnp.arange(TOKENS), side="right").astype(jnp.int32)
    gain = jnp.clip(1.0 + 0.18 * jax.random.normal(keys[7], (D,), jnp.float32), 0.1, 1.9)
    return dict(q_in=q_in, k_in=k_in, v_in=v_in, fir=fir, skip=skip, taps=taps, segments=segments, gain=gain)


def toeplitz(taps_row, row_pos, row_seg, col_pos, col_seg):
    offsets = row_pos[:, None] - col_pos[None, :]
    allowed = (offsets >= 0) & (row_seg[:, None] == col_seg[None, :])
    entries = jnp.take(taps_row, jnp.clip(offsets, 0, taps_row.shape[0] - 1).astype(jnp.int32))
    return jnp.where(allowed, entries, jnp.zeros((), taps_row.dtype))

def reference(q_in, k_in, v_in, fir, skip, taps, segments, gain):
    stacked = jnp.stack([q_in, k_in, v_in]).astype(jnp.float32)
    padded = jnp.pad(stacked, ((0, 0), (2, 0), (0, 0)))
    filtered = fir[:, 0, None, :] * padded[:, 2:] + fir[:, 1, None, :] * padded[:, 1:-1] + fir[:, 2, None, :] * padded[:, :-2]
    product_kv = (filtered[1] * filtered[2]).astype(jnp.bfloat16)
    nblock = TOKENS // TOK_DEV
    seg_blocks = segments.reshape(nblock, TOK_DEV)
    local_pos = jnp.arange(TOK_DEV, dtype=jnp.int32)
    kv_groups = product_kv.reshape(TOKENS, FG, GW).transpose(1, 0, 2)

    def one_group(pair):
        taps_row, kv_group = pair
        kv_blocks = kv_group.reshape(nblock, TOK_DEV, GW)

        def one_block(block):
            row_pos = (block * TOK_DEV + local_pos).astype(jnp.int32)
            row_seg = seg_blocks[block]

            def add_source(source, running):
                col_seg = seg_blocks[source]
                col_pos = (source * TOK_DEV + local_pos).astype(jnp.int32)

                def work(total):
                    matrix = toeplitz(taps_row, row_pos, row_seg, col_pos, col_seg)
                    return total + jnp.dot(matrix, kv_blocks[source], preferred_element_type=jnp.float32)
                return lax.cond(col_seg[-1] >= row_seg[0], work, lambda total: total, running)
            return lax.fori_loop(0, block + 1, add_source, jnp.zeros((TOK_DEV, GW), jnp.float32))
        return lax.map(one_block, jnp.arange(nblock, dtype=jnp.int32)).reshape(TOKENS, GW)
    conv = lax.map(one_group, (taps, kv_groups)).transpose(1, 0, 2).reshape(TOKENS, D)
    gated = filtered[0] * (conv + skip * product_kv.astype(jnp.float32))
    squares = lax.optimization_barrier(jnp.sum(gated * gated, axis=1, keepdims=True))
    mixed = gated * lax.rsqrt(squares / D + 1e-06) * gain
    return mixed.astype(jnp.bfloat16)
```

```python
import functools

import jax
import jax.numpy as jnp
from jax import lax
from jax.experimental import pallas as pl
from jax.experimental.pallas import tpu as pltpu
from jax.sharding import PartitionSpec as P

D = 8192
GW = 128
F32 = jnp.float32
BF16 = jnp.bfloat16
MESH = pl.DeviceIdType.MESH


def lagged(x, by, rows):
    return jnp.where(rows >= by, pltpu.roll(x, by, 0), 0.0)


def kernel(
    n, m, groups,
    q_hbm, k_hbm, v_hbm, fir, skip, taps, seg, gain, out,
    qbuf, kbuf, vbuf, own, slots, aux, fixes, mats, acc, fq, sqs,
    in_sem, aux_send, aux_recv, kv_send, kv_recv, fwd_send, sq_send, sq_recv,
):
    me, gi = lax.axis_index("ctx"), lax.axis_index("grp")
    tokens, width = qbuf.shape
    far = n - 2
    relay = n == 4

    barrier = pltpu.get_barrier_semaphore()
    for d in range(1, n):
        pl.semaphore_signal(barrier, inc=1, device_id={"ctx": lax.rem(me + d, n)}, device_id_type=MESH)
    for e in range(1, m):
        pl.semaphore_signal(barrier, inc=1, device_id={"grp": lax.rem(gi + e, m)}, device_id_type=MESH)
    loads = [
        pltpu.make_async_copy(src, dst, in_sem.at[i])
        for i, (src, dst) in enumerate(((k_hbm, kbuf), (v_hbm, vbuf), (q_hbm, qbuf)))
    ]
    for load in loads:
        load.start()

    def aux_copy(d, peer):
        return pltpu.make_async_remote_copy(
            src_ref=aux.at[0], dst_ref=aux.at[d], send_sem=aux_send.at[d - 1], recv_sem=aux_recv.at[d - 1],
            device_id={"ctx": peer}, device_id_type=MESH)

    def kv_copy(d, g, peer):
        return pltpu.make_async_remote_copy(
            src_ref=own.at[g], dst_ref=slots.at[d - 1, g], send_sem=kv_send.at[d - 1, g],
            recv_sem=kv_recv.at[d - 1, g], device_id={"ctx": peer}, device_id_type=MESH)

    def forward(g):
        return pltpu.make_async_remote_copy(
            src_ref=slots.at[1, g], dst_ref=slots.at[0, g], send_sem=fwd_send.at[g],
            recv_sem=kv_recv.at[0, g], device_id={"ctx": 2}, device_id_type=MESH)

    def sends(d):
        there = me + d < n
        return there & (me != 1) if relay and d == 1 else there

    rows = lax.broadcasted_iota(jnp.int32, (tokens, GW), 0)
    cols = lax.broadcasted_iota(jnp.int32, (tokens, GW), 1)
    row8 = lax.broadcasted_iota(jnp.int32, (8, width), 0)
    for load in loads:
        load.wait()

    def last8(ref):
        return ref[tokens - 16 :, :].astype(F32)[8:]

    def first8(ref):
        return ref[:16, :].astype(F32)[:8]

    seg_f = seg[...].astype(F32)
    seg_tile = jnp.concatenate([jnp.broadcast_to(seg_f, (8, GW))] * groups, axis=1)
    upper = jnp.where(
        row8 < 4,
        jnp.where(row8 < 2, pltpu.roll(last8(kbuf), 2, 0), pltpu.roll(first8(kbuf), 2, 0)),
        jnp.where(row8 < 6, pltpu.roll(last8(vbuf), 6, 0), pltpu.roll(first8(vbuf), 6, 0)))
    lower = jnp.where(row8 < 2, pltpu.roll(last8(qbuf), 2, 0), seg_tile)
    aux[0] = jnp.concatenate([upper, lower], axis=0).astype(BF16)

    pl.semaphore_wait(barrier, n - 1 + m - 1)
    for d in range(1, n):
        @pl.when(me + d < n)
        def _():
            aux_copy(d, me + d).start()

    for g in range(groups):
        lane = slice(g * GW, (g + 1) * GW)

        def filtered(ref, a):
            x = ref[:, lane].astype(F32)
            return (fir[a, 0:1, lane] * x + fir[a, 1:2, lane] * lagged(x, 1, rows)
                    + fir[a, 2:3, lane] * lagged(x, 2, rows))

        own[g] = (filtered(kbuf, 1) * filtered(vbuf, 2)).astype(BF16)
        for d in range(1, far + 1):
            @pl.when(sends(d))
            def _():
                kv_copy(d, g, me + d).start()

    for d in range(1, n):
        @pl.when(me >= d)
        def _():
            aux_copy(d, me - d).wait_recv()

    for d in range(far + 1):
        @pl.when(me - d >= 1)
        def _():
            before, after = aux[d + 1].astype(F32)[:8], aux[d].astype(F32)[:8]
            edge = jnp.where(lax.rem(row8, 4) < 2, before, after)
            tap = [jnp.where(row8 < 4, fir[1, i : i + 1, :], fir[2, i : i + 1, :]) for i in range(3)]
            both = tap[0] * edge + tap[1] * pltpu.roll(edge, 1, 0) + tap[2] * pltpu.roll(edge, 2, 0)
            fixes[d] = pltpu.roll(both * pltpu.roll(both, 4, 0), 6, 0)

    def block_of(ref, d, g):
        lane = slice(g * GW, (g + 1) * GW)
        whole = ref[...]
        top = whole[:16].astype(F32)
        limit = jnp.where(me - d >= 1, 2, 0)
        head = jnp.where(row8[:, :GW] < limit, fixes[d, :, lane], top[:8])
        return jnp.concatenate([jnp.concatenate([head, top[8:]], axis=0).astype(BF16), whole[16:]], axis=0)

    flip = (rows + cols == GW - 1).astype(BF16)
    target = jnp.broadcast_to(seg_f, (tokens, GW)).T
    same = [aux[d].astype(F32)[10:11, :GW] == target for d in range(far + 1)]
    same[0] = same[0] & (cols <= rows)
    for d in range(far + 1):
        back = jnp.dot(taps[:, d * GW : (d + 1) * GW], flip, preferred_element_type=F32)
        for g in range(groups):
            turned = pltpu.roll(jnp.broadcast_to(back[g : g + 1], (tokens, GW)), 1, 1, stride=1, stride_axis=0)
            if d < far:
                mats[d + 1, g] = jnp.where(same[d + 1] & (cols > rows), turned, 0.0).astype(BF16)
            if d == 0:
                mats[0, g] = jnp.where(same[0], turned, 0.0).astype(BF16)
            else:
                mats[d, g] += jnp.where(same[d] & (cols <= rows), turned, 0.0).astype(BF16)

    for g in range(groups):
        lane = slice(g * GW, (g + 1) * GW)
        block = block_of(own.at[g], 0, g)
        acc[g] = jnp.dot(mats[0, g], block, preferred_element_type=F32) + skip[:, lane] * block.astype(F32)
        x = qbuf[:, lane].astype(F32)
        halo = jnp.where(me >= 1, aux[1, :, lane].astype(F32), 0.0)
        one = jnp.where(rows < 1, halo[9:10], pltpu.roll(x, 1, 0))
        two = jnp.where(rows < 1, halo[8:9], jnp.where(rows < 2, halo[9:10], pltpu.roll(x, 2, 0)))
        fq[g] = fir[0, 0:1, lane] * x + fir[0, 1:2, lane] * one + fir[0, 2:3, lane] * two

    squares = jnp.zeros((tokens, GW), F32)
    for g in range(groups):
        for d in range(far, 0, -1):
            @pl.when(me >= d)
            def _():
                kv_copy(d, g, me - d).wait_recv()
                if relay and d == 2:
                    @pl.when(me == 3)
                    def _():
                        forward(g).start()
                acc[g] += jnp.dot(mats[d, g], block_of(slots.at[d - 1, g], d, g), preferred_element_type=F32)
        gated = fq[g] * acc[g]
        acc[g] = gated
        squares += gated * gated

    sqs[0] = jnp.sum(squares.T.reshape(GW // 8, 8, tokens), axis=0)

    def sq_copy(e, peer):
        return pltpu.make_async_remote_copy(
            src_ref=sqs.at[0], dst_ref=sqs.at[e], send_sem=sq_send.at[e - 1], recv_sem=sq_recv.at[e - 1],
            device_id={"grp": peer}, device_id_type=MESH)

    for e in range(1, m):
        sq_copy(e, lax.rem(gi + e, m)).start()
    for e in range(1, m):
        sq_copy(e, lax.rem(gi + m - e, m)).wait_recv()
    total = sqs[0]
    for e in range(1, m):
        total += sqs[e]
    scale = lax.rsqrt(jnp.sum(total, axis=0, keepdims=True) / D + 1e-06)
    scale = jnp.broadcast_to(scale, (GW, tokens)).T
    for g in range(groups):
        lane = slice(g * GW, (g + 1) * GW)
        out[:, lane] = (acc[g] * scale * gain[:, lane]).astype(BF16)

    for e in range(1, m):
        sq_copy(e, lax.rem(gi + e, m)).wait_send()
    for d in range(1, n):
        @pl.when(me + d < n)
        def _():
            aux_copy(d, me + d).wait_send()
    for d in range(1, far + 1):
        @pl.when(sends(d))
        def _():
            for g in range(groups):
                kv_copy(d, g, me + d).wait_send()
    if relay:
        @pl.when(me == 3)
        def _():
            for g in range(groups):
                forward(g).wait_send()


def on_device(n, m, q_in, k_in, v_in, fir, skip, taps, segments, gain):
    tokens, width = q_in.shape
    groups = width // GW
    far = n - 2
    vmem = pl.BlockSpec(memory_space=pltpu.VMEM)
    hbm = pl.BlockSpec(memory_space=pl.ANY)
    block = (groups, tokens, GW)
    dma = pltpu.SemaphoreType.DMA
    return pl.pallas_call(
        functools.partial(kernel, n, m, groups),
        out_shape=jax.ShapeDtypeStruct((tokens, width), BF16),
        in_specs=[hbm] * 3 + [vmem] * 5,
        out_specs=vmem,
        scratch_shapes=[
            pltpu.VMEM((tokens, width), BF16),
            pltpu.VMEM((tokens, width), BF16),
            pltpu.VMEM((tokens, width), BF16),
            pltpu.VMEM(block, BF16),
            pltpu.VMEM((far,) + block, BF16),
            pltpu.VMEM((n, 16, width), BF16),
            pltpu.VMEM((far + 1, 8, width), F32),
            pltpu.VMEM((far + 1,) + block, BF16),
            pltpu.VMEM(block, F32),
            pltpu.VMEM(block, F32),
            pltpu.VMEM((m, 8, tokens), F32),
            dma((3,)),
            dma((n - 1,)),
            dma((n - 1,)),
            dma((far, groups)),
            dma((far, groups)),
            dma((groups,)),
            dma((m - 1,)),
            dma((m - 1,)),
        ],
        compiler_params=pltpu.CompilerParams(
            collective_id=0, has_side_effects=True, vmem_limit_bytes=40 * 1024 * 1024
        ),
        cost_estimate=pl.CostEstimate(
            flops=2 * tokens * tokens * width * (far + 1), bytes_accessed=8 * tokens * width, transcendentals=0
        ),
        name="mixer",
    )(q_in, k_in, v_in, fir, skip[None, :], taps, segments[None, :], gain[None, :])


def solution(mesh):
    return jax.shard_map(
        functools.partial(on_device, mesh.shape["ctx"], mesh.shape["grp"]),
        mesh=mesh,
        in_specs=(
            P("ctx", "grp"),
            P("ctx", "grp"),
            P("ctx", "grp"),
            P(None, None, "grp"),
            P("grp"),
            P("grp", None),
            P("ctx"),
            P("grp"),
        ),
        out_specs=P("ctx", "grp"),
        check_vma=False,
    )
```

```python
import functools

import jax
import jax.numpy as jnp
from jax import lax
from jax.experimental import pallas as pl
from jax.experimental.pallas import tpu as pltpu
from jax.sharding import PartitionSpec as P

D = 8192
GW = 128
F32 = jnp.float32
BF16 = jnp.bfloat16
MESH = pl.DeviceIdType.MESH


def lagged(x, by, rows):
    return jnp.where(rows >= by, pltpu.roll(x, by, 0), 0.0)


def kernel(
    n, m, groups,
    q_hbm, k_hbm, v_hbm, fir_hbm, skip_hbm, taps_hbm, seg_hbm, gain_hbm, out,
    qbuf, kbuf, vbuf, fir, skip, taps, seg, gain, own, slots, aux, fixes, mats, acc, sqs,
    in_sem, aux_send, aux_recv, kv_send, kv_recv, fwd_send, sq_send, sq_recv,
):
    me, gi = lax.axis_index("ctx"), lax.axis_index("grp")
    tokens, width = qbuf.shape
    far = n - 2
    relay = n == 4

    pairs = (
        (k_hbm, kbuf), (v_hbm, vbuf), (q_hbm, qbuf), (fir_hbm, fir),
        (seg_hbm, seg), (taps_hbm, taps), (skip_hbm, skip), (gain_hbm, gain),
    )
    loads = [pltpu.make_async_copy(src, dst, in_sem.at[i]) for i, (src, dst) in enumerate(pairs)]
    for load in loads:
        load.start()
    barrier = pltpu.get_barrier_semaphore()
    for d in range(1, n):
        pl.semaphore_signal(barrier, inc=1, device_id={"ctx": lax.rem(me + d, n)}, device_id_type=MESH)
    for e in range(1, m):
        pl.semaphore_signal(barrier, inc=1, device_id={"grp": lax.rem(gi + e, m)}, device_id_type=MESH)
    def aux_copy(d, peer):
        return pltpu.make_async_remote_copy(
            src_ref=aux.at[0], dst_ref=aux.at[d], send_sem=aux_send.at[d - 1], recv_sem=aux_recv.at[d - 1],
            device_id={"ctx": peer}, device_id_type=MESH)

    def kv_copy(d, g, peer):
        return pltpu.make_async_remote_copy(
            src_ref=own.at[g], dst_ref=slots.at[d - 1, g], send_sem=kv_send.at[d - 1, g],
            recv_sem=kv_recv.at[d - 1, g], device_id={"ctx": peer}, device_id_type=MESH)

    def forward(g):
        return pltpu.make_async_remote_copy(
            src_ref=slots.at[1, g], dst_ref=slots.at[0, g], send_sem=fwd_send.at[g],
            recv_sem=kv_recv.at[0, g], device_id={"ctx": 2}, device_id_type=MESH)

    def sends(d):
        there = me + d < n
        return there & (me != 1) if relay and d == 1 else there

    rows = lax.broadcasted_iota(jnp.int32, (tokens, GW), 0)
    cols = lax.broadcasted_iota(jnp.int32, (tokens, GW), 1)
    row8 = lax.broadcasted_iota(jnp.int32, (8, width), 0)
    for load in loads:
        load.wait()

    def last8(ref):
        return ref[tokens - 16 :, :].astype(F32)[8:]

    def first8(ref):
        return ref[:16, :].astype(F32)[:8]

    seg_f = seg[...].astype(F32)
    seg_tile = jnp.concatenate([jnp.broadcast_to(seg_f, (8, GW))] * groups, axis=1)
    upper = jnp.where(
        row8 < 4,
        jnp.where(row8 < 2, pltpu.roll(last8(kbuf), 2, 0), pltpu.roll(first8(kbuf), 2, 0)),
        jnp.where(row8 < 6, pltpu.roll(last8(vbuf), 6, 0), pltpu.roll(first8(vbuf), 6, 0)))
    lower = jnp.where(row8 < 2, pltpu.roll(last8(qbuf), 2, 0), seg_tile)
    aux[0] = jnp.concatenate([upper, lower], axis=0).astype(BF16)

    def product(g):
        lane = slice(g * GW, (g + 1) * GW)

        def filtered(ref, a):
            x = ref[:, lane].astype(F32)
            return (fir[a, 0:1, lane] * x + fir[a, 1:2, lane] * lagged(x, 1, rows)
                    + fir[a, 2:3, lane] * lagged(x, 2, rows))

        own[g] = (filtered(kbuf, 1) * filtered(vbuf, 2)).astype(BF16)

    def send_chunk(g):
        for d in range(1, far + 1):
            @pl.when(sends(d))
            def _():
                kv_copy(d, g, me + d).start()

    product(0)
    pl.semaphore_wait(barrier, n - 1 + m - 1)
    for d in range(1, n):
        @pl.when(me + d < n)
        def _():
            aux_copy(d, me + d).start()
    send_chunk(0)
    for g in range(1, groups):
        product(g)
        send_chunk(g)

    for d in range(1, n):
        @pl.when(me >= d)
        def _():
            aux_copy(d, me - d).wait_recv()

    for d in range(far + 1):
        @pl.when(me - d >= 1)
        def _():
            before, after = aux[d + 1].astype(F32)[:8], aux[d].astype(F32)[:8]
            edge = jnp.where(lax.rem(row8, 4) < 2, before, after)
            tap = [jnp.where(row8 < 4, fir[1, i : i + 1, :], fir[2, i : i + 1, :]) for i in range(3)]
            both = tap[0] * edge + tap[1] * pltpu.roll(edge, 1, 0) + tap[2] * pltpu.roll(edge, 2, 0)
            fixes[d] = pltpu.roll(both * pltpu.roll(both, 4, 0), 6, 0)

    def block_of(ref, d, g):
        lane = slice(g * GW, (g + 1) * GW)
        whole = ref[...]
        top = whole[:16].astype(F32)
        limit = jnp.where(me - d >= 1, 2, 0)
        head = jnp.where(row8[:, :GW] < limit, fixes[d, :, lane], top[:8])
        return jnp.concatenate([jnp.concatenate([head, top[8:]], axis=0).astype(BF16), whole[16:]], axis=0)

    flip = (rows + cols == GW - 1).astype(BF16)
    target = jnp.broadcast_to(seg_f, (tokens, GW)).T
    back = [
        jnp.dot(taps[:, d * GW : (d + 1) * GW], flip, preferred_element_type=F32) for d in range(far + 1)
    ]

    def matrices(g):
        nearer = 0.0
        for d in range(far + 1):
            turned = pltpu.roll(jnp.broadcast_to(back[d][g : g + 1], (tokens, GW)), 1, 1, stride=1, stride_axis=0)
            same = aux[d].astype(F32)[10:11, :GW] == target
            mats[d] = jnp.where(same, jnp.where(cols <= rows, turned, nearer), 0.0).astype(BF16)
            nearer = turned

    squares = jnp.zeros((tokens, GW), F32)
    for g in range(groups):
        lane = slice(g * GW, (g + 1) * GW)
        matrices(g)
        block = block_of(own.at[g], 0, g)
        acc[g] = jnp.dot(mats[0], block, preferred_element_type=F32) + skip[:, lane] * block.astype(F32)
        x = qbuf[:, lane].astype(F32)
        halo = jnp.where(me >= 1, aux[1, :, lane].astype(F32), 0.0)
        one = jnp.where(rows < 1, halo[9:10], pltpu.roll(x, 1, 0))
        two = jnp.where(rows < 1, halo[8:9], jnp.where(rows < 2, halo[9:10], pltpu.roll(x, 2, 0)))
        query = fir[0, 0:1, lane] * x + fir[0, 1:2, lane] * one + fir[0, 2:3, lane] * two
        for d in range(far, 0, -1):
            @pl.when(me >= d)
            def _():
                kv_copy(d, g, me - d).wait_recv()
                if relay and d == 2:
                    @pl.when(me == 3)
                    def _():
                        forward(g).start()
                acc[g] += jnp.dot(mats[d], block_of(slots.at[d - 1, g], d, g), preferred_element_type=F32)
        gated = query * acc[g]
        acc[g] = gated
        squares += gated * gated

    sqs[0] = jnp.sum(squares.T.reshape(GW // 8, 8, tokens), axis=0)

    def sq_copy(e, peer):
        return pltpu.make_async_remote_copy(
            src_ref=sqs.at[0], dst_ref=sqs.at[e], send_sem=sq_send.at[e - 1], recv_sem=sq_recv.at[e - 1],
            device_id={"grp": peer}, device_id_type=MESH)

    for e in range(1, m):
        sq_copy(e, lax.rem(gi + e, m)).start()
    for e in range(1, m):
        sq_copy(e, lax.rem(gi + m - e, m)).wait_recv()
    total = sqs[0]
    for e in range(1, m):
        total += sqs[e]
    scale = lax.rsqrt(jnp.sum(total, axis=0, keepdims=True) / D + 1e-06)
    scale = jnp.broadcast_to(scale, (GW, tokens)).T
    for g in range(groups):
        lane = slice(g * GW, (g + 1) * GW)
        out[:, lane] = (acc[g] * scale * gain[:, lane]).astype(BF16)

    for e in range(1, m):
        sq_copy(e, lax.rem(gi + e, m)).wait_send()
    for d in range(1, n):
        @pl.when(me + d < n)
        def _():
            aux_copy(d, me + d).wait_send()
    for d in range(1, far + 1):
        @pl.when(sends(d))
        def _():
            for g in range(groups):
                kv_copy(d, g, me + d).wait_send()
    if relay:
        @pl.when(me == 3)
        def _():
            for g in range(groups):
                forward(g).wait_send()


def on_device(n, m, q_in, k_in, v_in, fir, skip, taps, segments, gain):
    tokens, width = q_in.shape
    groups = width // GW
    far = n - 2
    vmem = pl.BlockSpec(memory_space=pltpu.VMEM)
    hbm = pl.BlockSpec(memory_space=pltpu.HBM)
    block = (groups, tokens, GW)
    dma = pltpu.SemaphoreType.DMA
    return pl.pallas_call(
        functools.partial(kernel, n, m, groups),
        out_shape=jax.ShapeDtypeStruct((tokens, width), BF16),
        in_specs=[hbm] * 8,
        out_specs=vmem,
        scratch_shapes=[
            pltpu.VMEM((tokens, width), BF16),
            pltpu.VMEM((tokens, width), BF16),
            pltpu.VMEM((tokens, width), BF16),
            pltpu.VMEM(fir.shape, F32),
            pltpu.VMEM((1, width), F32),
            pltpu.VMEM(taps.shape, BF16),
            pltpu.VMEM((1, tokens), jnp.int32),
            pltpu.VMEM((1, width), F32),
            pltpu.VMEM(block, BF16),
            pltpu.VMEM((far,) + block, BF16),
            pltpu.VMEM((n, 16, width), BF16),
            pltpu.VMEM((far + 1, 8, width), F32),
            pltpu.VMEM((far + 1, tokens, GW), BF16),
            pltpu.VMEM(block, F32),
            pltpu.VMEM((m, 8, tokens), F32),
            dma((8,)),
            dma((n - 1,)),
            dma((n - 1,)),
            dma((far, groups)),
            dma((far, groups)),
            dma((groups,)),
            dma((m - 1,)),
            dma((m - 1,)),
        ],
        compiler_params=pltpu.CompilerParams(
            collective_id=0, has_side_effects=True, vmem_limit_bytes=63 * 1024 * 1024
        ),
        cost_estimate=pl.CostEstimate(
            flops=2 * tokens * tokens * width * (far + 1), bytes_accessed=8 * tokens * width, transcendentals=0
        ),
        name="mixer",
    )(q_in, k_in, v_in, fir, skip[None, :], taps, segments[None, :], gain[None, :])


def solution(mesh):
    return jax.shard_map(
        functools.partial(on_device, mesh.shape["ctx"], mesh.shape["grp"]),
        mesh=mesh,
        in_specs=(
            P("ctx", "grp"),
            P("ctx", "grp"),
            P("ctx", "grp"),
            P(None, None, "grp"),
            P("grp"),
            P("grp", None),
            P("ctx"),
            P("grp"),
        ),
        out_specs=P("ctx", "grp"),
        check_vma=False,
    )
```

```python
import functools

import jax
import jax.numpy as jnp
from jax import lax
from jax.experimental import pallas as pl
from jax.experimental.pallas import tpu as pltpu
from jax.sharding import PartitionSpec as P

D = 8192
GW = 128
F32 = jnp.float32
BF16 = jnp.bfloat16
MESH = pl.DeviceIdType.MESH


def lagged(x, by, rows):
    return jnp.where(rows >= by, pltpu.roll(x, by, 0), 0.0)


def kernel(
    n, m, groups,
    q_hbm, k_hbm, v_hbm, fir_hbm, skip_hbm, taps_hbm, seg_hbm, gain_hbm, out,
    qbuf, kbuf, vbuf, fir, skip, taps, seg, gain, own, slots, aux, fixes, mats, acc, sqs,
    in_sem, aux_send, aux_recv, kv_send, kv_recv, fwd_send, sq_send, sq_recv,
):
    me, gi = lax.axis_index("ctx"), lax.axis_index("grp")
    tokens, width = qbuf.shape
    far = n - 2
    relay = n == 4
    relayed = groups - max(1, groups // 4)
    ahead = 2

    pairs = (
        (k_hbm, kbuf), (v_hbm, vbuf), (q_hbm, qbuf), (fir_hbm, fir),
        (seg_hbm, seg), (taps_hbm, taps), (skip_hbm, skip), (gain_hbm, gain),
    )
    loads = [pltpu.make_async_copy(src, dst, in_sem.at[i]) for i, (src, dst) in enumerate(pairs)]
    for load in loads:
        load.start()
    barrier = pltpu.get_barrier_semaphore()
    for d in range(1, n):
        pl.semaphore_signal(barrier, inc=1, device_id={"ctx": lax.rem(me + d, n)}, device_id_type=MESH)
    for e in range(1, m):
        pl.semaphore_signal(barrier, inc=1, device_id={"grp": lax.rem(gi + e, m)}, device_id_type=MESH)
    def aux_copy(d, peer):
        return pltpu.make_async_remote_copy(
            src_ref=aux.at[0], dst_ref=aux.at[d], send_sem=aux_send.at[d - 1], recv_sem=aux_recv.at[d - 1],
            device_id={"ctx": peer}, device_id_type=MESH)

    def kv_copy(d, g, peer):
        return pltpu.make_async_remote_copy(
            src_ref=own.at[g], dst_ref=slots.at[d - 1, g], send_sem=kv_send.at[d - 1, g],
            recv_sem=kv_recv.at[d - 1, g], device_id={"ctx": peer}, device_id_type=MESH)

    def forward(g):
        return pltpu.make_async_remote_copy(
            src_ref=slots.at[1, g], dst_ref=slots.at[0, g], send_sem=fwd_send.at[g],
            recv_sem=kv_recv.at[0, g], device_id={"ctx": 2}, device_id_type=MESH)

    def sends(d, g):
        there = me + d < n
        return there & (me != 1) if relay and d == 1 and g < relayed else there

    def pass_on(g):
        if relay and g < relayed:
            @pl.when(me == 3)
            def _():
                kv_copy(2, g, 1).wait_recv()
                forward(g).start()

    rows = lax.broadcasted_iota(jnp.int32, (tokens, GW), 0)
    cols = lax.broadcasted_iota(jnp.int32, (tokens, GW), 1)
    row8 = lax.broadcasted_iota(jnp.int32, (8, width), 0)
    for load in loads:
        load.wait()

    def last8(ref):
        return ref[tokens - 16 :, :].astype(F32)[8:]

    def first8(ref):
        return ref[:16, :].astype(F32)[:8]

    seg_f = seg[...].astype(F32)
    seg_tile = jnp.concatenate([jnp.broadcast_to(seg_f, (8, GW))] * groups, axis=1)
    upper = jnp.where(
        row8 < 4,
        jnp.where(row8 < 2, pltpu.roll(last8(kbuf), 2, 0), pltpu.roll(first8(kbuf), 2, 0)),
        jnp.where(row8 < 6, pltpu.roll(last8(vbuf), 6, 0), pltpu.roll(first8(vbuf), 6, 0)))
    lower = jnp.where(row8 < 2, pltpu.roll(last8(qbuf), 2, 0), seg_tile)
    aux[0] = jnp.concatenate([upper, lower], axis=0).astype(BF16)

    def product(g):
        lane = slice(g * GW, (g + 1) * GW)

        def filtered(ref, a):
            x = ref[:, lane].astype(F32)
            return (fir[a, 0:1, lane] * x + fir[a, 1:2, lane] * lagged(x, 1, rows)
                    + fir[a, 2:3, lane] * lagged(x, 2, rows))

        own[g] = (filtered(kbuf, 1) * filtered(vbuf, 2)).astype(BF16)

    def send_chunk(g):
        for d in range(1, far + 1):
            @pl.when(sends(d, g))
            def _():
                kv_copy(d, g, me + d).start()

    product(0)
    pl.semaphore_wait(barrier, n - 1 + m - 1)
    for d in range(1, n):
        @pl.when(me + d < n)
        def _():
            aux_copy(d, me + d).start()
    send_chunk(0)
    for g in range(1, groups):
        product(g)
        send_chunk(g)

    for d in range(1, n):
        @pl.when(me >= d)
        def _():
            aux_copy(d, me - d).wait_recv()

    for d in range(far + 1):
        @pl.when(me - d >= 1)
        def _():
            before, after = aux[d + 1].astype(F32)[:8], aux[d].astype(F32)[:8]
            edge = jnp.where(lax.rem(row8, 4) < 2, before, after)
            tap = [jnp.where(row8 < 4, fir[1, i : i + 1, :], fir[2, i : i + 1, :]) for i in range(3)]
            both = tap[0] * edge + tap[1] * pltpu.roll(edge, 1, 0) + tap[2] * pltpu.roll(edge, 2, 0)
            fixes[d] = pltpu.roll(both * pltpu.roll(both, 4, 0), 6, 0)

    def block_of(ref, d, g):
        lane = slice(g * GW, (g + 1) * GW)
        whole = ref[...]
        top = whole[:16].astype(F32)
        limit = jnp.where(me - d >= 1, 2, 0)
        head = jnp.where(row8[:, :GW] < limit, fixes[d, :, lane], top[:8])
        return jnp.concatenate([jnp.concatenate([head, top[8:]], axis=0).astype(BF16), whole[16:]], axis=0)

    flip = (rows + cols == GW - 1).astype(BF16)
    target = jnp.broadcast_to(seg_f, (tokens, GW)).T
    back = [
        jnp.dot(taps[:, d * GW : (d + 1) * GW], flip, preferred_element_type=F32) for d in range(far + 1)
    ]

    def matrices(g):
        nearer = 0.0
        for d in range(far + 1):
            turned = pltpu.roll(jnp.broadcast_to(back[d][g : g + 1], (tokens, GW)), 1, 1, stride=1, stride_axis=0)
            same = aux[d].astype(F32)[10:11, :GW] == target
            mats[d] = jnp.where(same, jnp.where(cols <= rows, turned, nearer), 0.0).astype(BF16)
            nearer = turned

    squares = jnp.zeros((tokens, GW), F32)
    for g in range(ahead):
        pass_on(g)
    for g in range(groups):
        lane = slice(g * GW, (g + 1) * GW)
        pass_on(g + ahead)
        matrices(g)
        block = block_of(own.at[g], 0, g)
        acc[g] = jnp.dot(mats[0], block, preferred_element_type=F32) + skip[:, lane] * block.astype(F32)
        x = qbuf[:, lane].astype(F32)
        halo = jnp.where(me >= 1, aux[1, :, lane].astype(F32), 0.0)
        one = jnp.where(rows < 1, halo[9:10], pltpu.roll(x, 1, 0))
        two = jnp.where(rows < 1, halo[8:9], jnp.where(rows < 2, halo[9:10], pltpu.roll(x, 2, 0)))
        query = fir[0, 0:1, lane] * x + fir[0, 1:2, lane] * one + fir[0, 2:3, lane] * two
        for d in range(far, 0, -1):
            @pl.when(me >= d)
            def _():
                if relay and d == 2 and g < relayed:
                    @pl.when(me == 2)
                    def _():
                        kv_copy(d, g, me - d).wait_recv()
                else:
                    kv_copy(d, g, me - d).wait_recv()
                acc[g] += jnp.dot(mats[d], block_of(slots.at[d - 1, g], d, g), preferred_element_type=F32)
        gated = query * acc[g]
        acc[g] = gated
        squares += gated * gated

    sqs[0] = jnp.sum(squares.T.reshape(GW // 8, 8, tokens), axis=0)

    def sq_copy(e, peer):
        return pltpu.make_async_remote_copy(
            src_ref=sqs.at[0], dst_ref=sqs.at[e], send_sem=sq_send.at[e - 1], recv_sem=sq_recv.at[e - 1],
            device_id={"grp": peer}, device_id_type=MESH)

    for e in range(1, m):
        sq_copy(e, lax.rem(gi + e, m)).start()
    for e in range(1, m):
        sq_copy(e, lax.rem(gi + m - e, m)).wait_recv()
    total = sqs[0]
    for e in range(1, m):
        total += sqs[e]
    scale = lax.rsqrt(jnp.sum(total, axis=0, keepdims=True) / D + 1e-06)
    scale = jnp.broadcast_to(scale, (GW, tokens)).T
    for g in range(groups):
        lane = slice(g * GW, (g + 1) * GW)
        out[:, lane] = (acc[g] * scale * gain[:, lane]).astype(BF16)

    for e in range(1, m):
        sq_copy(e, lax.rem(gi + e, m)).wait_send()
    for d in range(1, n):
        @pl.when(me + d < n)
        def _():
            aux_copy(d, me + d).wait_send()
    for d in range(1, far + 1):
        for g in range(groups):
            @pl.when(sends(d, g))
            def _():
                kv_copy(d, g, me + d).wait_send()
    if relay:
        @pl.when(me == 3)
        def _():
            for g in range(relayed):
                forward(g).wait_send()


def on_device(n, m, q_in, k_in, v_in, fir, skip, taps, segments, gain):
    tokens, width = q_in.shape
    groups = width // GW
    far = n - 2
    vmem = pl.BlockSpec(memory_space=pltpu.VMEM)
    hbm = pl.BlockSpec(memory_space=pltpu.HBM)
    block = (groups, tokens, GW)
    dma = pltpu.SemaphoreType.DMA
    return pl.pallas_call(
        functools.partial(kernel, n, m, groups),
        out_shape=pltpu.VMEM((tokens, width), BF16),
        in_specs=[hbm] * 8,
        out_specs=vmem,
        scratch_shapes=[
            pltpu.VMEM((tokens, width), BF16),
            pltpu.VMEM((tokens, width), BF16),
            pltpu.VMEM((tokens, width), BF16),
            pltpu.VMEM(fir.shape, F32),
            pltpu.VMEM((1, width), F32),
            pltpu.VMEM(taps.shape, BF16),
            pltpu.VMEM((1, tokens), jnp.int32),
            pltpu.VMEM((1, width), F32),
            pltpu.VMEM(block, BF16),
            pltpu.VMEM((far,) + block, BF16),
            pltpu.VMEM((n, 16, width), BF16),
            pltpu.VMEM((far + 1, 8, width), F32),
            pltpu.VMEM((far + 1, tokens, GW), BF16),
            pltpu.VMEM(block, F32),
            pltpu.VMEM((m, 8, tokens), F32),
            dma((8,)),
            dma((n - 1,)),
            dma((n - 1,)),
            dma((far, groups)),
            dma((far, groups)),
            dma((groups,)),
            dma((m - 1,)),
            dma((m - 1,)),
        ],
        compiler_params=pltpu.CompilerParams(
            collective_id=0, has_side_effects=True, vmem_limit_bytes=40 * 1024 * 1024
        ),
        cost_estimate=pl.CostEstimate(
            flops=2 * tokens * tokens * width * (far + 1), bytes_accessed=8 * tokens * width, transcendentals=0
        ),
        name="mixer",
    )(*[
        pltpu.with_memory_space_constraint(x, pltpu.HBM)
        for x in (q_in, k_in, v_in, fir, skip[None, :], taps, segments[None, :], gain[None, :])
    ])


def solution(mesh):
    return jax.shard_map(
        functools.partial(on_device, mesh.shape["ctx"], mesh.shape["grp"]),
        mesh=mesh,
        in_specs=(
            P("ctx", "grp"),
            P("ctx", "grp"),
            P("ctx", "grp"),
            P(None, None, "grp"),
            P("grp"),
            P("grp", None),
            P("ctx"),
            P("grp"),
        ),
        out_specs=P("ctx", "grp"),
        check_vma=False,
    )
```

```python
import functools

import jax
import jax.numpy as jnp
from jax import lax
from jax.experimental import pallas as pl
from jax.experimental.pallas import tpu as pltpu
from jax.sharding import PartitionSpec as P

D = 8192
GW = 128
F32 = jnp.float32
BF16 = jnp.bfloat16
MESH = pl.DeviceIdType.MESH


def lagged(x, by, rows):
    return jnp.where(rows >= by, pltpu.roll(x, by, 0), 0.0)


def kernel(
    n, m, groups,
    q_hbm, k_hbm, v_hbm, fir_hbm, skip_hbm, taps_hbm, seg_hbm, gain_hbm, out,
    qbuf, kbuf, vbuf, fir, skip, taps, seg, gain, own, slots, halo, edges, mats, acc, sqs,
    in_sem, halo_sem, edge_send, edge_recv, kv_send, kv_recv, fwd_send, sq_send, sq_recv,
):
    me, gi = lax.axis_index("ctx"), lax.axis_index("grp")
    tokens, width = qbuf.shape
    far = n - 2
    relay = n == 4
    relayed = groups - max(1, groups // 8)
    ahead = 2

    pairs = (
        (k_hbm, kbuf), (v_hbm, vbuf), (q_hbm, qbuf), (fir_hbm, fir),
        (seg_hbm, seg), (taps_hbm, taps), (skip_hbm, skip), (gain_hbm, gain),
    )
    loads = [pltpu.make_async_copy(src, dst, in_sem.at[i]) for i, (src, dst) in enumerate(pairs)]
    for load in loads:
        load.start()
    barrier = pltpu.get_barrier_semaphore()
    for d in range(1, n):
        pl.semaphore_signal(barrier, inc=1, device_id={"ctx": lax.rem(me + d, n)}, device_id_type=MESH)
    for e in range(1, m):
        pl.semaphore_signal(barrier, inc=1, device_id={"grp": lax.rem(gi + e, m)}, device_id_type=MESH)
    def halo_copy(peer):
        return pltpu.make_async_remote_copy(
            src_ref=halo.at[0], dst_ref=halo.at[1], send_sem=halo_sem.at[0], recv_sem=halo_sem.at[1],
            device_id={"ctx": peer}, device_id_type=MESH)

    def edge_copy(d, peer):
        return pltpu.make_async_remote_copy(
            src_ref=edges.at[0], dst_ref=edges.at[d], send_sem=edge_send.at[d - 1], recv_sem=edge_recv.at[d - 1],
            device_id={"ctx": peer}, device_id_type=MESH)

    def kv_copy(d, g, peer):
        return pltpu.make_async_remote_copy(
            src_ref=own.at[g], dst_ref=slots.at[d - 1, g], send_sem=kv_send.at[d - 1, g],
            recv_sem=kv_recv.at[d - 1, g], device_id={"ctx": peer}, device_id_type=MESH)

    def forward(g):
        return pltpu.make_async_remote_copy(
            src_ref=slots.at[1, g], dst_ref=slots.at[0, g], send_sem=fwd_send.at[g],
            recv_sem=kv_recv.at[0, g], device_id={"ctx": 2}, device_id_type=MESH)

    def sends(d, g):
        there = me + d < n
        return there & (me != 1) if relay and d == 1 and g < relayed else there

    def pass_on(g):
        if relay and g < relayed:
            @pl.when(me == 3)
            def _():
                kv_copy(2, g, 1).wait_recv()
                forward(g).start()

    rows = lax.broadcasted_iota(jnp.int32, (tokens, GW), 0)
    cols = lax.broadcasted_iota(jnp.int32, (tokens, GW), 1)
    row8 = lax.broadcasted_iota(jnp.int32, (8, width), 0)
    for load in loads:
        load.wait()

    def last8(ref, by):
        return pltpu.roll(ref[tokens - 16 :, :].astype(F32)[8:], by, 0)

    def first8(ref, by):
        return pltpu.roll(ref[:16, :].astype(F32)[:8], by, 0)

    half = width // 2
    last = jnp.where(row8 < 2, last8(kbuf, 2), jnp.where(row8 < 4, last8(qbuf, 4), last8(vbuf, 6)))
    halo[0] = jnp.concatenate([last[:, :half], last[:, half:]], axis=0).astype(BF16)

    def product(g):
        lane = slice(g * GW, (g + 1) * GW)

        def filtered(ref, a):
            x = ref[:, lane].astype(F32)
            return (fir[a, 0:1, lane] * x + fir[a, 1:2, lane] * lagged(x, 1, rows)
                    + fir[a, 2:3, lane] * lagged(x, 2, rows))

        own[g] = (filtered(kbuf, 1) * filtered(vbuf, 2)).astype(BF16)

    def send_chunk(g):
        for d in range(1, far + 1):
            @pl.when(sends(d, g))
            def _():
                kv_copy(d, g, me + d).start()

    product(0)
    pl.semaphore_wait(barrier, n - 1 + m - 1)
    @pl.when(me + 1 < n)
    def _():
        halo_copy(me + 1).start()

    send_chunk(0)
    early = min(3, groups)
    for g in range(1, early):
        product(g)
        send_chunk(g)

    @pl.when(me >= 1)
    def _():
        halo_copy(me - 1).wait_recv()

    before = halo[1].astype(F32)
    before = jnp.where(me >= 1, jnp.concatenate([before[:8], before[8:]], axis=1), 0.0)
    edge = jnp.where(
        lax.rem(row8, 4) < 2, before, jnp.where(row8 < 4, first8(kbuf, 2), first8(vbuf, 6)))
    tap = [jnp.where(row8 < 4, fir[1, i : i + 1, :], fir[2, i : i + 1, :]) for i in range(3)]
    both = tap[0] * edge + tap[1] * pltpu.roll(edge, 1, 0) + tap[2] * pltpu.roll(edge, 2, 0)
    fix = pltpu.roll(both * pltpu.roll(both, 4, 0), 6, 0)
    small8 = row8[:, :GW]
    folded = [jnp.zeros((8, GW), F32)] * 2
    for g in range(groups):
        t, j = g // 4, 2 * (g % 4)
        piece = fix[:, g * GW : (g + 1) * GW]
        piece = pltpu.roll(piece, j, 0) if j else piece
        folded[t] = jnp.where((small8 >= j) & (small8 < j + 2), piece, folded[t])
    seg_f = seg[...].astype(F32)
    edges[0] = jnp.concatenate(
        [jnp.concatenate(folded, axis=0), jnp.broadcast_to(seg_f, (16, GW))], axis=1).astype(BF16)
    for d in range(1, far + 1):
        @pl.when(me + d < n)
        def _():
            edge_copy(d, me + d).start()
    for g in range(early, groups):
        product(g)
        send_chunk(g)
    for d in range(1, far + 1):
        @pl.when(me >= d)
        def _():
            edge_copy(d, me - d).wait_recv()

    def block_of(ref, d, g):
        t, j = g // 4, 2 * (g % 4)
        first = edges[d].astype(F32)[8 * t : 8 * t + 8, :GW]
        first = pltpu.roll(first, 8 - j, 0) if j else first
        whole = ref[...]
        top = whole[:16].astype(F32)
        head = jnp.concatenate([jnp.where(small8 < 2, first, top[:8]), top[8:]], axis=0)
        return jnp.concatenate([head.astype(BF16), whole[16:]], axis=0)

    flip = (rows + cols == GW - 1).astype(BF16)
    target = jnp.broadcast_to(seg_f, (tokens, GW)).T
    back = [
        jnp.dot(taps[:, d * GW : (d + 1) * GW], flip, preferred_element_type=F32) for d in range(far + 1)
    ]

    def matrices(g):
        nearer = 0.0
        for d in range(far + 1):
            turned = pltpu.roll(jnp.broadcast_to(back[d][g : g + 1], (tokens, GW)), 1, 1, stride=1, stride_axis=0)
            same = edges[d].astype(F32)[:1, GW:] == target
            mats[d] = jnp.where(same, jnp.where(cols <= rows, turned, nearer), 0.0).astype(BF16)
            nearer = turned

    squares = jnp.zeros((tokens, GW), F32)
    for g in range(ahead):
        pass_on(g)
    for g in range(groups):
        lane = slice(g * GW, (g + 1) * GW)
        pass_on(g + ahead)
        matrices(g)
        block = block_of(own.at[g], 0, g)
        acc[g] = jnp.dot(mats[0], block, preferred_element_type=F32) + skip[:, lane] * block.astype(F32)
        x = qbuf[:, lane].astype(F32)
        one = jnp.where(rows < 1, before[3:4, lane], pltpu.roll(x, 1, 0))
        two = jnp.where(rows < 1, before[2:3, lane], jnp.where(rows < 2, before[3:4, lane], pltpu.roll(x, 2, 0)))
        query = fir[0, 0:1, lane] * x + fir[0, 1:2, lane] * one + fir[0, 2:3, lane] * two
        for d in range(far, 0, -1):
            @pl.when(me >= d)
            def _():
                if relay and d == 2 and g < relayed:
                    @pl.when(me == 2)
                    def _():
                        kv_copy(d, g, me - d).wait_recv()
                else:
                    kv_copy(d, g, me - d).wait_recv()
                acc[g] += jnp.dot(mats[d], block_of(slots.at[d - 1, g], d, g), preferred_element_type=F32)
        gated = query * acc[g]
        acc[g] = gated
        squares += gated * gated

    sqs[0] = jnp.sum(squares.T.reshape(GW // 8, 8, tokens), axis=0)

    def sq_copy(e, peer):
        return pltpu.make_async_remote_copy(
            src_ref=sqs.at[0], dst_ref=sqs.at[e], send_sem=sq_send.at[e - 1], recv_sem=sq_recv.at[e - 1],
            device_id={"grp": peer}, device_id_type=MESH)

    for e in range(1, m):
        sq_copy(e, lax.rem(gi + e, m)).start()
    for e in range(1, m):
        sq_copy(e, lax.rem(gi + m - e, m)).wait_recv()
    total = sqs[0]
    for e in range(1, m):
        total += sqs[e]
    scale = lax.rsqrt(jnp.sum(total, axis=0, keepdims=True) / D + 1e-06)
    scale = jnp.broadcast_to(scale, (GW, tokens)).T
    for g in range(groups):
        lane = slice(g * GW, (g + 1) * GW)
        out[:, lane] = (acc[g] * scale * gain[:, lane]).astype(BF16)

    for e in range(1, m):
        sq_copy(e, lax.rem(gi + e, m)).wait_send()
    @pl.when(me + 1 < n)
    def _():
        halo_copy(me + 1).wait_send()

    for d in range(1, far + 1):
        @pl.when(me + d < n)
        def _():
            edge_copy(d, me + d).wait_send()
    for d in range(1, far + 1):
        for g in range(groups):
            @pl.when(sends(d, g))
            def _():
                kv_copy(d, g, me + d).wait_send()
    if relay:
        @pl.when(me == 3)
        def _():
            for g in range(relayed):
                forward(g).wait_send()


def on_device(n, m, q_in, k_in, v_in, fir, skip, taps, segments, gain):
    tokens, width = q_in.shape
    groups = width // GW
    far = n - 2
    vmem = pl.BlockSpec(memory_space=pltpu.VMEM)
    hbm = pl.BlockSpec(memory_space=pltpu.HBM)
    block = (groups, tokens, GW)
    dma = pltpu.SemaphoreType.DMA
    return pl.pallas_call(
        functools.partial(kernel, n, m, groups),
        out_shape=pltpu.VMEM((tokens, width), BF16),
        in_specs=[hbm] * 8,
        out_specs=vmem,
        scratch_shapes=[
            pltpu.VMEM((tokens, width), BF16),
            pltpu.VMEM((tokens, width), BF16),
            pltpu.VMEM((tokens, width), BF16),
            pltpu.VMEM(fir.shape, F32),
            pltpu.VMEM((1, width), F32),
            pltpu.VMEM(taps.shape, BF16),
            pltpu.VMEM((1, tokens), jnp.int32),
            pltpu.VMEM((1, width), F32),
            pltpu.VMEM(block, BF16),
            pltpu.VMEM((far,) + block, BF16),
            pltpu.VMEM((2, 16, width // 2), BF16),
            pltpu.VMEM((far + 1, 16, 2 * GW), BF16),
            pltpu.VMEM((far + 1, tokens, GW), BF16),
            pltpu.VMEM(block, F32),
            pltpu.VMEM((m, 8, tokens), F32),
            dma((8,)),
            dma((2,)),
            dma((far,)),
            dma((far,)),
            dma((far, groups)),
            dma((far, groups)),
            dma((groups,)),
            dma((m - 1,)),
            dma((m - 1,)),
        ],
        compiler_params=pltpu.CompilerParams(
            collective_id=0, has_side_effects=True, vmem_limit_bytes=40 * 1024 * 1024
        ),
        cost_estimate=pl.CostEstimate(
            flops=2 * tokens * tokens * width * (far + 1), bytes_accessed=8 * tokens * width, transcendentals=0
        ),
        name="mixer",
    )(*[
        pltpu.with_memory_space_constraint(x, pltpu.HBM)
        for x in (q_in, k_in, v_in, fir, skip[None, :], taps, segments[None, :], gain[None, :])
    ])


def solution(mesh):
    return jax.shard_map(
        functools.partial(on_device, mesh.shape["ctx"], mesh.shape["grp"]),
        mesh=mesh,
        in_specs=(
            P("ctx", "grp"),
            P("ctx", "grp"),
            P("ctx", "grp"),
            P(None, None, "grp"),
            P("grp"),
            P("grp", None),
            P("ctx"),
            P("grp"),
        ),
        out_specs=P("ctx", "grp"),
        check_vma=False,
    )
```

```python
import functools

import jax
import jax.numpy as jnp
from jax import lax
from jax.experimental import pallas as pl
from jax.experimental.pallas import tpu as pltpu
from jax.sharding import PartitionSpec as P

D = 8192
GW = 128
F32 = jnp.float32
BF16 = jnp.bfloat16
MESH = pl.DeviceIdType.MESH


def lagged(x, by, rows):
    return jnp.where(rows >= by, pltpu.roll(x, by, 0), 0.0)


def kernel(
    n, m, groups,
    q_hbm, k_hbm, v_hbm, fir_hbm, skip_hbm, taps_hbm, seg_hbm, gain_hbm, out,
    qbuf, kbuf, vbuf, fir, skip, taps, seg, gain, own, slots, halo, edges, mats, masks, acc, fq, sqs,
    in_sem, halo_sem, edge_send, edge_recv, kv_send, kv_recv, fwd_send, sq_send, sq_recv,
):
    me, gi = lax.axis_index("ctx"), lax.axis_index("grp")
    tokens, width = qbuf.shape
    far = n - 2
    relay = n == 4
    relayed = groups - max(1, groups // 8)

    pairs = (
        (k_hbm, kbuf), (v_hbm, vbuf), (q_hbm, qbuf), (fir_hbm, fir),
        (seg_hbm, seg), (taps_hbm, taps), (skip_hbm, skip), (gain_hbm, gain),
    )
    loads = [pltpu.make_async_copy(src, dst, in_sem.at[i]) for i, (src, dst) in enumerate(pairs)]
    for load in loads:
        load.start()
    barrier = pltpu.get_barrier_semaphore()
    for d in range(1, n):
        pl.semaphore_signal(barrier, inc=1, device_id={"ctx": lax.rem(me + d, n)}, device_id_type=MESH)
    for e in range(1, m):
        pl.semaphore_signal(barrier, inc=1, device_id={"grp": lax.rem(gi + e, m)}, device_id_type=MESH)
    def halo_copy(peer):
        return pltpu.make_async_remote_copy(
            src_ref=halo.at[0], dst_ref=halo.at[1], send_sem=halo_sem.at[0], recv_sem=halo_sem.at[1],
            device_id={"ctx": peer}, device_id_type=MESH)

    def edge_copy(d, peer):
        return pltpu.make_async_remote_copy(
            src_ref=edges.at[0], dst_ref=edges.at[d], send_sem=edge_send.at[d - 1], recv_sem=edge_recv.at[d - 1],
            device_id={"ctx": peer}, device_id_type=MESH)

    def kv_copy(d, g, peer):
        return pltpu.make_async_remote_copy(
            src_ref=own.at[g], dst_ref=slots.at[d - 1, g], send_sem=kv_send.at[d - 1, g],
            recv_sem=kv_recv.at[d - 1, g], device_id={"ctx": peer}, device_id_type=MESH)

    def forward(g):
        return pltpu.make_async_remote_copy(
            src_ref=slots.at[1, g], dst_ref=slots.at[0, g], send_sem=fwd_send.at[g],
            recv_sem=kv_recv.at[0, g], device_id={"ctx": 2}, device_id_type=MESH)

    def sends(d, g):
        there = me + d < n
        return there & (me != 1) if relay and d == 1 and g < relayed else there

    def pass_on(g):
        if relay and g < relayed:
            @pl.when(me == 3)
            def _():
                kv_copy(2, g, 1).wait_recv()
                forward(g).start()

    rows = lax.broadcasted_iota(jnp.int32, (tokens, GW), 0)
    cols = lax.broadcasted_iota(jnp.int32, (tokens, GW), 1)
    row8 = lax.broadcasted_iota(jnp.int32, (8, width), 0)
    for load in loads:
        load.wait()

    def last8(ref, by):
        return pltpu.roll(ref[tokens - 16 :, :].astype(F32)[8:], by, 0)

    def first8(ref, by):
        return pltpu.roll(ref[:16, :].astype(F32)[:8], by, 0)

    half = width // 2
    last = jnp.where(row8 < 2, last8(kbuf, 2), jnp.where(row8 < 4, last8(qbuf, 4), last8(vbuf, 6)))
    halo[0] = jnp.concatenate([last[:, :half], last[:, half:]], axis=0).astype(BF16)

    def product(g):
        lane = slice(g * GW, (g + 1) * GW)

        def filtered(ref, a):
            x = ref[:, lane].astype(F32)
            return (fir[a, 0:1, lane] * x + fir[a, 1:2, lane] * lagged(x, 1, rows)
                    + fir[a, 2:3, lane] * lagged(x, 2, rows))

        own[g] = (filtered(kbuf, 1) * filtered(vbuf, 2)).astype(BF16)

    def send_chunk(g):
        for d in range(1, far + 1):
            @pl.when(sends(d, g))
            def _():
                kv_copy(d, g, me + d).start()

    product(0)
    pl.semaphore_wait(barrier, n - 1 + m - 1)
    @pl.when(me + 1 < n)
    def _():
        halo_copy(me + 1).start()

    send_chunk(0)
    early = min(3, groups)
    for g in range(1, early):
        product(g)
        send_chunk(g)

    @pl.when(me >= 1)
    def _():
        halo_copy(me - 1).wait_recv()

    before = halo[1].astype(F32)
    before = jnp.where(me >= 1, jnp.concatenate([before[:8], before[8:]], axis=1), 0.0)
    edge = jnp.where(
        lax.rem(row8, 4) < 2, before, jnp.where(row8 < 4, first8(kbuf, 2), first8(vbuf, 6)))
    tap = [jnp.where(row8 < 4, fir[1, i : i + 1, :], fir[2, i : i + 1, :]) for i in range(3)]
    both = tap[0] * edge + tap[1] * pltpu.roll(edge, 1, 0) + tap[2] * pltpu.roll(edge, 2, 0)
    fix = pltpu.roll(both * pltpu.roll(both, 4, 0), 6, 0)
    small8 = row8[:, :GW]
    folded = [jnp.zeros((8, GW), F32)] * 2
    for g in range(groups):
        t, j = g // 4, 2 * (g % 4)
        piece = fix[:, g * GW : (g + 1) * GW]
        piece = pltpu.roll(piece, j, 0) if j else piece
        folded[t] = jnp.where((small8 >= j) & (small8 < j + 2), piece, folded[t])
    seg_f = seg[...].astype(F32)
    edges[0] = jnp.concatenate(
        [jnp.concatenate(folded, axis=0), jnp.broadcast_to(seg_f, (16, GW))], axis=1).astype(BF16)
    for d in range(1, far + 1):
        @pl.when(me + d < n)
        def _():
            edge_copy(d, me + d).start()
    passed = 0
    for g in range(early, groups):
        product(g)
        send_chunk(g)
        if g >= early + 2:
            pass_on(passed)
            passed += 1

    def block_of(ref, d, g):
        t, j = g // 4, 2 * (g % 4)
        first = edges[d].astype(F32)[8 * t : 8 * t + 8, :GW]
        first = pltpu.roll(first, 8 - j, 0) if j else first
        whole = ref[...]
        top = whole[:16].astype(F32)
        head = jnp.concatenate([jnp.where(small8 < 2, first, top[:8]), top[8:]], axis=0)
        return jnp.concatenate([head.astype(BF16), whole[16:]], axis=0)

    flip = (rows + cols == GW - 1).astype(BF16)
    target = jnp.broadcast_to(seg_f, (tokens, GW)).T

    def mask(d):
        return jnp.where(edges[d].astype(F32)[:1, GW:] == target, 1.0, 0.0).astype(BF16)

    masks[0] = mask(0)
    back = [
        jnp.dot(taps[:, d * GW : (d + 1) * GW], flip, preferred_element_type=F32) for d in range(far + 1)
    ]
    for g in range(groups):
        lane = slice(g * GW, (g + 1) * GW)
        nearer = 0.0
        for d in range(far + 1):
            turned = pltpu.roll(jnp.broadcast_to(back[d][g : g + 1], (tokens, GW)), 1, 1, stride=1, stride_axis=0)
            mats[d, g] = jnp.where(cols <= rows, turned, nearer).astype(BF16)
            nearer = turned
        block = block_of(own.at[g], 0, g)
        acc[g] = (jnp.dot(mats[0, g] * masks[0], block, preferred_element_type=F32)
                  + skip[:, lane] * block.astype(F32))
        x = qbuf[:, lane].astype(F32)
        one = jnp.where(rows < 1, before[3:4, lane], pltpu.roll(x, 1, 0))
        two = jnp.where(rows < 1, before[2:3, lane], jnp.where(rows < 2, before[3:4, lane], pltpu.roll(x, 2, 0)))
        fq[g] = fir[0, 0:1, lane] * x + fir[0, 1:2, lane] * one + fir[0, 2:3, lane] * two
        if g % 4 == 3:
            pass_on(passed)
            passed += 1

    for d in range(1, far + 1):
        @pl.when(me >= d)
        def _():
            edge_copy(d, me - d).wait_recv()
            masks[d] = mask(d)

    squares = jnp.zeros((tokens, GW), F32)
    for g in range(groups):
        pass_on(passed)
        passed += 1
        for d in range(far, 0, -1):
            @pl.when(me >= d)
            def _():
                if relay and d == 2 and g < relayed:
                    @pl.when(me == 2)
                    def _():
                        kv_copy(d, g, me - d).wait_recv()
                else:
                    kv_copy(d, g, me - d).wait_recv()
                acc[g] += jnp.dot(
                    mats[d, g] * masks[d], block_of(slots.at[d - 1, g], d, g), preferred_element_type=F32)
        gated = fq[g] * acc[g]
        acc[g] = gated
        squares += gated * gated

    sqs[0] = jnp.sum(squares.T.reshape(GW // 8, 8, tokens), axis=0)

    def sq_copy(e, peer):
        return pltpu.make_async_remote_copy(
            src_ref=sqs.at[0], dst_ref=sqs.at[e], send_sem=sq_send.at[e - 1], recv_sem=sq_recv.at[e - 1],
            device_id={"grp": peer}, device_id_type=MESH)

    for e in range(1, m):
        sq_copy(e, lax.rem(gi + e, m)).start()
    for e in range(1, m):
        sq_copy(e, lax.rem(gi + m - e, m)).wait_recv()
    total = sqs[0]
    for e in range(1, m):
        total += sqs[e]
    scale = lax.rsqrt(jnp.sum(total, axis=0, keepdims=True) / D + 1e-06)
    scale = jnp.broadcast_to(scale, (GW, tokens)).T
    for g in range(groups):
        lane = slice(g * GW, (g + 1) * GW)
        out[:, lane] = (acc[g] * scale * gain[:, lane]).astype(BF16)

    for e in range(1, m):
        sq_copy(e, lax.rem(gi + e, m)).wait_send()
    @pl.when(me + 1 < n)
    def _():
        halo_copy(me + 1).wait_send()

    for d in range(1, far + 1):
        @pl.when(me + d < n)
        def _():
            edge_copy(d, me + d).wait_send()
    for d in range(1, far + 1):
        for g in range(groups):
            @pl.when(sends(d, g))
            def _():
                kv_copy(d, g, me + d).wait_send()
    if relay:
        @pl.when(me == 3)
        def _():
            for g in range(relayed):
                forward(g).wait_send()


def on_device(n, m, q_in, k_in, v_in, fir, skip, taps, segments, gain):
    tokens, width = q_in.shape
    groups = width // GW
    far = n - 2
    vmem = pl.BlockSpec(memory_space=pltpu.VMEM)
    hbm = pl.BlockSpec(memory_space=pltpu.HBM)
    block = (groups, tokens, GW)
    dma = pltpu.SemaphoreType.DMA
    return pl.pallas_call(
        functools.partial(kernel, n, m, groups),
        out_shape=pltpu.VMEM((tokens, width), BF16),
        in_specs=[hbm] * 8,
        out_specs=vmem,
        scratch_shapes=[
            pltpu.VMEM((tokens, width), BF16),
            pltpu.VMEM((tokens, width), BF16),
            pltpu.VMEM((tokens, width), BF16),
            pltpu.VMEM(fir.shape, F32),
            pltpu.VMEM((1, width), F32),
            pltpu.VMEM(taps.shape, BF16),
            pltpu.VMEM((1, tokens), jnp.int32),
            pltpu.VMEM((1, width), F32),
            pltpu.VMEM(block, BF16),
            pltpu.VMEM((far,) + block, BF16),
            pltpu.VMEM((2, 16, width // 2), BF16),
            pltpu.VMEM((far + 1, 16, 2 * GW), BF16),
            pltpu.VMEM((far + 1,) + block, BF16),
            pltpu.VMEM((far + 1, tokens, GW), BF16),
            pltpu.VMEM(block, F32),
            pltpu.VMEM(block, F32),
            pltpu.VMEM((m, 8, tokens), F32),
            dma((8,)),
            dma((2,)),
            dma((far,)),
            dma((far,)),
            dma((far, groups)),
            dma((far, groups)),
            dma((groups,)),
            dma((m - 1,)),
            dma((m - 1,)),
        ],
        compiler_params=pltpu.CompilerParams(
            collective_id=0, has_side_effects=True, vmem_limit_bytes=40 * 1024 * 1024
        ),
        cost_estimate=pl.CostEstimate(
            flops=2 * tokens * tokens * width * (far + 1), bytes_accessed=8 * tokens * width, transcendentals=0
        ),
        name="mixer",
    )(*[
        pltpu.with_memory_space_constraint(x, pltpu.HBM)
        for x in (q_in, k_in, v_in, fir, skip[None, :], taps, segments[None, :], gain[None, :])
    ])


def solution(mesh):
    return jax.shard_map(
        functools.partial(on_device, mesh.shape["ctx"], mesh.shape["grp"]),
        mesh=mesh,
        in_specs=(
            P("ctx", "grp"),
            P("ctx", "grp"),
            P("ctx", "grp"),
            P(None, None, "grp"),
            P("grp"),
            P("grp", None),
            P("ctx"),
            P("grp"),
        ),
        out_specs=P("ctx", "grp"),
        check_vma=False,
    )
```

```python
import functools

import jax
import jax.numpy as jnp
from jax import lax
from jax.experimental import pallas as pl
from jax.experimental.pallas import tpu as pltpu
from jax.sharding import PartitionSpec as P

D = 8192
GW = 128
F32 = jnp.float32
BF16 = jnp.bfloat16
MESH = pl.DeviceIdType.MESH


def lagged(x, by, rows):
    return jnp.where(rows >= by, pltpu.roll(x, by, 0), 0.0)


def kernel(
    n, m, groups,
    q_hbm, k_hbm, v_hbm, fir_hbm, skip_hbm, taps_hbm, seg_hbm, gain_hbm, out,
    qbuf, kbuf, vbuf, fir, skip, taps, seg, gain, own, slots, halo, edges, mats, masks, acc, fq, sqs,
    in_sem, halo_sem, edge_send, edge_recv, kv_send, kv_recv, fwd_send, sq_send, sq_recv,
):
    me, gi = lax.axis_index("ctx"), lax.axis_index("grp")
    tokens, width = qbuf.shape
    far = n - 2
    relay = n == 4
    relayed = groups - max(1, groups // 8)

    pairs = (
        (k_hbm, kbuf), (v_hbm, vbuf), (q_hbm, qbuf), (fir_hbm, fir),
        (seg_hbm, seg), (taps_hbm, taps), (skip_hbm, skip), (gain_hbm, gain),
    )
    loads = [pltpu.make_async_copy(src, dst, in_sem.at[i]) for i, (src, dst) in enumerate(pairs)]
    for load in loads:
        load.start()
    barrier = pltpu.get_barrier_semaphore()
    for d in range(1, n):
        pl.semaphore_signal(barrier, inc=1, device_id={"ctx": lax.rem(me + d, n)}, device_id_type=MESH)
    for e in range(1, m):
        pl.semaphore_signal(barrier, inc=1, device_id={"grp": lax.rem(gi + e, m)}, device_id_type=MESH)
    def halo_copy(peer):
        return pltpu.make_async_remote_copy(
            src_ref=halo.at[0], dst_ref=halo.at[1], send_sem=halo_sem.at[0], recv_sem=halo_sem.at[1],
            device_id={"ctx": peer}, device_id_type=MESH)

    def edge_copy(d, peer):
        return pltpu.make_async_remote_copy(
            src_ref=edges.at[0], dst_ref=edges.at[d], send_sem=edge_send.at[d - 1], recv_sem=edge_recv.at[d - 1],
            device_id={"ctx": peer}, device_id_type=MESH)

    def kv_copy(d, g, peer):
        return pltpu.make_async_remote_copy(
            src_ref=own.at[g], dst_ref=slots.at[d - 1, g], send_sem=kv_send.at[d - 1, g],
            recv_sem=kv_recv.at[d - 1, g], device_id={"ctx": peer}, device_id_type=MESH)

    def forward(g):
        return pltpu.make_async_remote_copy(
            src_ref=slots.at[1, g], dst_ref=slots.at[0, g], send_sem=fwd_send.at[g],
            recv_sem=kv_recv.at[0, g], device_id={"ctx": 2}, device_id_type=MESH)

    def sends(d, g):
        there = me + d < n
        return there & (me != 1) if relay and d == 1 else there

    def pass_on(g):
        if relay and g < relayed:
            @pl.when(me == 3)
            def _():
                kv_copy(2, g, 1).wait_recv()
                forward(g).start()

    rows = lax.broadcasted_iota(jnp.int32, (tokens, GW), 0)
    cols = lax.broadcasted_iota(jnp.int32, (tokens, GW), 1)
    row8 = lax.broadcasted_iota(jnp.int32, (8, width), 0)
    for load in loads:
        load.wait()

    def last8(ref, by):
        return pltpu.roll(ref[tokens - 16 :, :].astype(F32)[8:], by, 0)

    def first8(ref, by):
        return pltpu.roll(ref[:16, :].astype(F32)[:8], by, 0)

    half = width // 2
    last = jnp.where(row8 < 2, last8(kbuf, 2), jnp.where(row8 < 4, last8(qbuf, 4), last8(vbuf, 6)))
    halo[0] = jnp.concatenate([last[:, :half], last[:, half:]], axis=0).astype(BF16)

    def product(g):
        lane = slice(g * GW, (g + 1) * GW)

        def filtered(ref, a):
            x = ref[:, lane].astype(F32)
            return (fir[a, 0:1, lane] * x + fir[a, 1:2, lane] * lagged(x, 1, rows)
                    + fir[a, 2:3, lane] * lagged(x, 2, rows))

        own[g] = (filtered(kbuf, 1) * filtered(vbuf, 2)).astype(BF16)

    def send_chunk(g):
        for d in range(far, 0, -1):
            @pl.when(sends(d, g))
            def _():
                kv_copy(d, g, me + d).start()

    direct = range(relayed, groups) if relay else range(0)
    for g in (*direct, 0):
        product(g)
    pl.semaphore_wait(barrier, n - 1 + m - 1)
    @pl.when(me + 1 < n)
    def _():
        halo_copy(me + 1).start()

    if relay:
        @pl.when(me == 1)
        def _():
            for g in direct:
                kv_copy(1, g, 2).start()

    send_chunk(0)
    early = min(3, groups)
    for g in range(1, early):
        product(g)
        send_chunk(g)

    @pl.when(me >= 1)
    def _():
        halo_copy(me - 1).wait_recv()

    before = halo[1].astype(F32)
    before = jnp.where(me >= 1, jnp.concatenate([before[:8], before[8:]], axis=1), 0.0)
    edge = jnp.where(
        lax.rem(row8, 4) < 2, before, jnp.where(row8 < 4, first8(kbuf, 2), first8(vbuf, 6)))
    tap = [jnp.where(row8 < 4, fir[1, i : i + 1, :], fir[2, i : i + 1, :]) for i in range(3)]
    both = tap[0] * edge + tap[1] * pltpu.roll(edge, 1, 0) + tap[2] * pltpu.roll(edge, 2, 0)
    fix = pltpu.roll(both * pltpu.roll(both, 4, 0), 6, 0)
    small8 = row8[:, :GW]
    folded = [jnp.zeros((8, GW), F32)] * 2
    for g in range(groups):
        t, j = g // 4, 2 * (g % 4)
        piece = fix[:, g * GW : (g + 1) * GW]
        piece = pltpu.roll(piece, j, 0) if j else piece
        folded[t] = jnp.where((small8 >= j) & (small8 < j + 2), piece, folded[t])
    seg_f = seg[...].astype(F32)
    edges[0] = jnp.concatenate(
        [jnp.concatenate(folded, axis=0), jnp.broadcast_to(seg_f, (16, GW))], axis=1).astype(BF16)
    for d in range(1, far + 1):
        @pl.when(me + d < n)
        def _():
            edge_copy(d, me + d).start()
    passed = 0
    for g in range(early, groups):
        if g not in direct:
            product(g)
        send_chunk(g)
        if g >= early + 2:
            pass_on(passed)
            passed += 1

    def block_of(ref, d, g):
        t, j = g // 4, 2 * (g % 4)
        first = edges[d].astype(F32)[8 * t : 8 * t + 8, :GW]
        first = pltpu.roll(first, 8 - j, 0) if j else first
        whole = ref[...]
        top = whole[:16].astype(F32)
        head = jnp.concatenate([jnp.where(small8 < 2, first, top[:8]), top[8:]], axis=0)
        return jnp.concatenate([head.astype(BF16), whole[16:]], axis=0)

    flip = (rows + cols == GW - 1).astype(BF16)
    target = jnp.broadcast_to(seg_f, (tokens, GW)).T

    def mask(d):
        return jnp.where(edges[d].astype(F32)[:1, GW:] == target, 1.0, 0.0).astype(BF16)

    masks[0] = mask(0)
    back = [
        jnp.dot(taps[:, d * GW : (d + 1) * GW], flip, preferred_element_type=F32) for d in range(far + 1)
    ]
    for g in range(groups):
        lane = slice(g * GW, (g + 1) * GW)
        nearer = 0.0
        for d in range(far + 1):
            turned = pltpu.roll(jnp.broadcast_to(back[d][g : g + 1], (tokens, GW)), 1, 1, stride=1, stride_axis=0)
            mats[d, g] = jnp.where(cols <= rows, turned, nearer).astype(BF16)
            nearer = turned
        block = block_of(own.at[g], 0, g)
        acc[g] = (jnp.dot(mats[0, g] * masks[0], block, preferred_element_type=F32)
                  + skip[:, lane] * block.astype(F32))
        x = qbuf[:, lane].astype(F32)
        one = jnp.where(rows < 1, before[3:4, lane], pltpu.roll(x, 1, 0))
        two = jnp.where(rows < 1, before[2:3, lane], jnp.where(rows < 2, before[3:4, lane], pltpu.roll(x, 2, 0)))
        fq[g] = fir[0, 0:1, lane] * x + fir[0, 1:2, lane] * one + fir[0, 2:3, lane] * two
        if g % 4 == 3:
            pass_on(passed)
            passed += 1

    for d in range(1, far + 1):
        @pl.when(me >= d)
        def _():
            edge_copy(d, me - d).wait_recv()
            masks[d] = mask(d)

    squares = jnp.zeros((tokens, GW), F32)
    for g in range(groups):
        pass_on(passed)
        passed += 1
        for d in range(far, 0, -1):
            @pl.when(me >= d)
            def _():
                if relay and d == 2 and g < relayed:
                    @pl.when(me == 2)
                    def _():
                        kv_copy(d, g, me - d).wait_recv()
                else:
                    kv_copy(d, g, me - d).wait_recv()
                acc[g] += jnp.dot(
                    mats[d, g] * masks[d], block_of(slots.at[d - 1, g], d, g), preferred_element_type=F32)
        gated = fq[g] * acc[g]
        acc[g] = gated
        squares += gated * gated

    sqs[0] = jnp.sum(squares.T.reshape(GW // 8, 8, tokens), axis=0)

    def sq_copy(e, peer):
        return pltpu.make_async_remote_copy(
            src_ref=sqs.at[0], dst_ref=sqs.at[e], send_sem=sq_send.at[e - 1], recv_sem=sq_recv.at[e - 1],
            device_id={"grp": peer}, device_id_type=MESH)

    for e in range(1, m):
        sq_copy(e, lax.rem(gi + e, m)).start()
    for e in range(1, m):
        sq_copy(e, lax.rem(gi + m - e, m)).wait_recv()
    total = sqs[0]
    for e in range(1, m):
        total += sqs[e]
    scale = lax.rsqrt(jnp.sum(total, axis=0, keepdims=True) / D + 1e-06)
    scale = jnp.broadcast_to(scale, (GW, tokens)).T
    for g in range(groups):
        lane = slice(g * GW, (g + 1) * GW)
        out[:, lane] = (acc[g] * scale * gain[:, lane]).astype(BF16)

    for e in range(1, m):
        sq_copy(e, lax.rem(gi + e, m)).wait_send()
    @pl.when(me + 1 < n)
    def _():
        halo_copy(me + 1).wait_send()

    for d in range(1, far + 1):
        @pl.when(me + d < n)
        def _():
            edge_copy(d, me + d).wait_send()
    for d in range(1, far + 1):
        for g in range(groups):
            @pl.when(sends(d, g))
            def _():
                kv_copy(d, g, me + d).wait_send()
    if relay:
        @pl.when(me == 1)
        def _():
            for g in direct:
                kv_copy(1, g, 2).wait_send()

        @pl.when(me == 3)
        def _():
            for g in range(relayed):
                forward(g).wait_send()


def on_device(n, m, q_in, k_in, v_in, fir, skip, taps, segments, gain):
    tokens, width = q_in.shape
    groups = width // GW
    far = n - 2
    vmem = pl.BlockSpec(memory_space=pltpu.VMEM)
    hbm = pl.BlockSpec(memory_space=pltpu.HBM)
    block = (groups, tokens, GW)
    dma = pltpu.SemaphoreType.DMA
    return pl.pallas_call(
        functools.partial(kernel, n, m, groups),
        out_shape=pltpu.VMEM((tokens, width), BF16),
        in_specs=[hbm] * 8,
        out_specs=vmem,
        scratch_shapes=[
            pltpu.VMEM((tokens, width), BF16),
            pltpu.VMEM((tokens, width), BF16),
            pltpu.VMEM((tokens, width), BF16),
            pltpu.VMEM(fir.shape, F32),
            pltpu.VMEM((1, width), F32),
            pltpu.VMEM(taps.shape, BF16),
            pltpu.VMEM((1, tokens), jnp.int32),
            pltpu.VMEM((1, width), F32),
            pltpu.VMEM(block, BF16),
            pltpu.VMEM((far,) + block, BF16),
            pltpu.VMEM((2, 16, width // 2), BF16),
            pltpu.VMEM((far + 1, 16, 2 * GW), BF16),
            pltpu.VMEM((far + 1,) + block, BF16),
            pltpu.VMEM((far + 1, tokens, GW), BF16),
            pltpu.VMEM(block, F32),
            pltpu.VMEM(block, F32),
            pltpu.VMEM((m, 8, tokens), F32),
            dma((8,)),
            dma((2,)),
            dma((far,)),
            dma((far,)),
            dma((far, groups)),
            dma((far, groups)),
            dma((groups,)),
            dma((m - 1,)),
            dma((m - 1,)),
        ],
        compiler_params=pltpu.CompilerParams(
            collective_id=0, has_side_effects=True, vmem_limit_bytes=40 * 1024 * 1024
        ),
        cost_estimate=pl.CostEstimate(
            flops=2 * tokens * tokens * width * (far + 1), bytes_accessed=8 * tokens * width, transcendentals=0
        ),
        name="mixer",
    )(*[
        pltpu.with_memory_space_constraint(x, pltpu.HBM)
        for x in (q_in, k_in, v_in, fir, skip[None, :], taps, segments[None, :], gain[None, :])
    ])


def solution(mesh):
    return jax.shard_map(
        functools.partial(on_device, mesh.shape["ctx"], mesh.shape["grp"]),
        mesh=mesh,
        in_specs=(
            P("ctx", "grp"),
            P("ctx", "grp"),
            P("ctx", "grp"),
            P(None, None, "grp"),
            P("grp"),
            P("grp", None),
            P("ctx"),
            P("grp"),
        ),
        out_specs=P("ctx", "grp"),
        check_vma=False,
    )
```

```python
import functools

import jax
import jax.numpy as jnp
from jax import lax
from jax.experimental import pallas as pl
from jax.experimental.pallas import tpu as pltpu
from jax.sharding import PartitionSpec as P

D = 8192
GW = 128
F32 = jnp.float32
BF16 = jnp.bfloat16
MESH = pl.DeviceIdType.MESH


def lagged(x, by, rows):
    return jnp.where(rows >= by, pltpu.roll(x, by, 0), 0.0)


def kernel(
    n, m, groups,
    q_hbm, k_hbm, v_hbm, fir_hbm, skip_hbm, taps_hbm, seg_hbm, gain_hbm, out,
    qbuf, kbuf, vbuf, fir, skip, taps, seg, gain, own, slots, halo, edges, mats, masks, acc, fq, sqs,
    in_sem, halo_sem, edge_send, edge_recv, kv_send, kv_recv, fwd_send, sq_send, sq_recv,
):
    me, gi = lax.axis_index("ctx"), lax.axis_index("grp")
    tokens, width = qbuf.shape
    far = n - 2
    relay = n == 4
    relayed = groups - max(1, groups // 4)

    pairs = (
        (k_hbm, kbuf), (v_hbm, vbuf), (q_hbm, qbuf), (fir_hbm, fir),
        (seg_hbm, seg), (taps_hbm, taps), (skip_hbm, skip), (gain_hbm, gain),
    )
    loads = [pltpu.make_async_copy(src, dst, in_sem.at[i]) for i, (src, dst) in enumerate(pairs)]
    for load in loads:
        load.start()
    barrier = pltpu.get_barrier_semaphore()
    for d in range(1, n):
        pl.semaphore_signal(barrier, inc=1, device_id={"ctx": lax.rem(me + d, n)}, device_id_type=MESH)
    for e in range(1, m):
        pl.semaphore_signal(barrier, inc=1, device_id={"grp": lax.rem(gi + e, m)}, device_id_type=MESH)
    def halo_copy(peer):
        return pltpu.make_async_remote_copy(
            src_ref=halo.at[0], dst_ref=halo.at[1], send_sem=halo_sem.at[0], recv_sem=halo_sem.at[1],
            device_id={"ctx": peer}, device_id_type=MESH)

    def edge_copy(d, peer):
        return pltpu.make_async_remote_copy(
            src_ref=edges.at[0], dst_ref=edges.at[d], send_sem=edge_send.at[d - 1], recv_sem=edge_recv.at[d - 1],
            device_id={"ctx": peer}, device_id_type=MESH)

    def kv_copy(d, g, peer):
        return pltpu.make_async_remote_copy(
            src_ref=own.at[g], dst_ref=slots.at[d - 1, g], send_sem=kv_send.at[d - 1, g],
            recv_sem=kv_recv.at[d - 1, g], device_id={"ctx": peer}, device_id_type=MESH)

    def forward(g):
        return pltpu.make_async_remote_copy(
            src_ref=slots.at[1, g], dst_ref=slots.at[0, g], send_sem=fwd_send.at[g],
            recv_sem=kv_recv.at[0, g], device_id={"ctx": 2}, device_id_type=MESH)

    def sends(d, g):
        there = me + d < n
        return there & (me != 1) if relay and d == 1 else there

    def pass_on(g):
        if relay and g < relayed:
            @pl.when(me == 3)
            def _():
                kv_copy(2, g, 1).wait_recv()
                forward(g).start()

    rows = lax.broadcasted_iota(jnp.int32, (tokens, GW), 0)
    cols = lax.broadcasted_iota(jnp.int32, (tokens, GW), 1)
    row8 = lax.broadcasted_iota(jnp.int32, (8, width), 0)
    for load in loads:
        load.wait()

    def last8(ref, by):
        return pltpu.roll(ref[tokens - 16 :, :].astype(F32)[8:], by, 0)

    def first8(ref, by):
        return pltpu.roll(ref[:16, :].astype(F32)[:8], by, 0)

    half = width // 2
    last = jnp.where(row8 < 2, last8(kbuf, 2), jnp.where(row8 < 4, last8(qbuf, 4), last8(vbuf, 6)))
    halo[0] = jnp.concatenate([last[:, :half], last[:, half:]], axis=0).astype(BF16)

    def product(g):
        lane = slice(g * GW, (g + 1) * GW)

        def filtered(ref, a):
            x = ref[:, lane].astype(F32)
            return (fir[a, 0:1, lane] * x + fir[a, 1:2, lane] * lagged(x, 1, rows)
                    + fir[a, 2:3, lane] * lagged(x, 2, rows))

        own[g] = (filtered(kbuf, 1) * filtered(vbuf, 2)).astype(BF16)

    def send_chunk(g):
        for d in range(far, 0, -1):
            @pl.when(sends(d, g))
            def _():
                kv_copy(d, g, me + d).start()

    direct = range(relayed, groups) if relay else range(0)
    for g in (*direct, 0):
        product(g)
    pl.semaphore_wait(barrier, n - 1 + m - 1)
    @pl.when(me + 1 < n)
    def _():
        halo_copy(me + 1).start()

    if relay:
        @pl.when(me == 1)
        def _():
            for g in direct:
                kv_copy(1, g, 2).start()

    send_chunk(0)
    early = min(3, groups)
    for g in range(1, early):
        product(g)
        send_chunk(g)

    @pl.when(me >= 1)
    def _():
        halo_copy(me - 1).wait_recv()

    before = halo[1].astype(F32)
    before = jnp.where(me >= 1, jnp.concatenate([before[:8], before[8:]], axis=1), 0.0)
    edge = jnp.where(
        lax.rem(row8, 4) < 2, before, jnp.where(row8 < 4, first8(kbuf, 2), first8(vbuf, 6)))
    tap = [jnp.where(row8 < 4, fir[1, i : i + 1, :], fir[2, i : i + 1, :]) for i in range(3)]
    both = tap[0] * edge + tap[1] * pltpu.roll(edge, 1, 0) + tap[2] * pltpu.roll(edge, 2, 0)
    fix = pltpu.roll(both * pltpu.roll(both, 4, 0), 6, 0)
    small8 = row8[:, :GW]
    folded = [jnp.zeros((8, GW), F32)] * 2
    for g in range(groups):
        t, j = g // 4, 2 * (g % 4)
        piece = fix[:, g * GW : (g + 1) * GW]
        piece = pltpu.roll(piece, j, 0) if j else piece
        folded[t] = jnp.where((small8 >= j) & (small8 < j + 2), piece, folded[t])
    seg_f = seg[...].astype(F32)
    edges[0] = jnp.concatenate(
        [jnp.concatenate(folded, axis=0), jnp.broadcast_to(seg_f, (16, GW))], axis=1).astype(BF16)
    for d in range(1, far + 1):
        @pl.when(me + d < n)
        def _():
            edge_copy(d, me + d).start()
    passed = 0
    for g in range(early, groups):
        if g not in direct:
            product(g)
        send_chunk(g)
        if g >= early + 2:
            pass_on(passed)
            passed += 1

    def block_of(ref, d, g):
        t, j = g // 4, 2 * (g % 4)
        first = edges[d].astype(F32)[8 * t : 8 * t + 8, :GW]
        first = pltpu.roll(first, 8 - j, 0) if j else first
        whole = ref[...]
        top = whole[:16].astype(F32)
        head = jnp.concatenate([jnp.where(small8 < 2, first, top[:8]), top[8:]], axis=0)
        return jnp.concatenate([head.astype(BF16), whole[16:]], axis=0)

    flip = (rows + cols == GW - 1).astype(BF16)
    target = jnp.broadcast_to(seg_f, (tokens, GW)).T

    def mask(d):
        return jnp.where(edges[d].astype(F32)[:1, GW:] == target, 1.0, 0.0).astype(BF16)

    masks[0] = mask(0)
    back = [
        jnp.dot(taps[:, d * GW : (d + 1) * GW], flip, preferred_element_type=F32) for d in range(far + 1)
    ]
    for g in range(groups):
        lane = slice(g * GW, (g + 1) * GW)
        nearer = 0.0
        for d in range(far + 1):
            turned = pltpu.roll(jnp.broadcast_to(back[d][g : g + 1], (tokens, GW)), 1, 1, stride=1, stride_axis=0)
            mats[d, g] = jnp.where(cols <= rows, turned, nearer).astype(BF16)
            nearer = turned
        block = block_of(own.at[g], 0, g)
        acc[g] = (jnp.dot(mats[0, g] * masks[0], block, preferred_element_type=F32)
                  + skip[:, lane] * block.astype(F32))
        x = qbuf[:, lane].astype(F32)
        one = jnp.where(rows < 1, before[3:4, lane], pltpu.roll(x, 1, 0))
        two = jnp.where(rows < 1, before[2:3, lane], jnp.where(rows < 2, before[3:4, lane], pltpu.roll(x, 2, 0)))
        fq[g] = fir[0, 0:1, lane] * x + fir[0, 1:2, lane] * one + fir[0, 2:3, lane] * two
        if g % 3 == 1:
            pass_on(passed)
            passed += 1

    for d in range(1, far + 1):
        @pl.when(me >= d)
        def _():
            edge_copy(d, me - d).wait_recv()
            masks[d] = mask(d)

    squares = jnp.zeros((tokens, GW), F32)
    for g in range(groups):
        pass_on(passed)
        passed += 1
        for d in range(far, 0, -1):
            @pl.when(me >= d)
            def _():
                if relay and d == 2 and g < relayed:
                    @pl.when(me == 2)
                    def _():
                        kv_copy(d, g, me - d).wait_recv()
                else:
                    kv_copy(d, g, me - d).wait_recv()
                acc[g] += jnp.dot(
                    mats[d, g] * masks[d], block_of(slots.at[d - 1, g], d, g), preferred_element_type=F32)
        gated = fq[g] * acc[g]
        acc[g] = gated
        squares += gated * gated

    sqs[0] = jnp.sum(squares.T.reshape(GW // 8, 8, tokens), axis=0)

    def sq_copy(e, peer):
        return pltpu.make_async_remote_copy(
            src_ref=sqs.at[0], dst_ref=sqs.at[e], send_sem=sq_send.at[e - 1], recv_sem=sq_recv.at[e - 1],
            device_id={"grp": peer}, device_id_type=MESH)

    for e in range(1, m):
        sq_copy(e, lax.rem(gi + e, m)).start()
    @pl.when(me + 1 < n)
    def _():
        halo_copy(me + 1).wait_send()

    for d in range(1, far + 1):
        @pl.when(me + d < n)
        def _():
            edge_copy(d, me + d).wait_send()
    for d in range(1, far + 1):
        for g in range(groups):
            @pl.when(sends(d, g))
            def _():
                kv_copy(d, g, me + d).wait_send()
    if relay:
        @pl.when(me == 1)
        def _():
            for g in direct:
                kv_copy(1, g, 2).wait_send()

        @pl.when(me == 3)
        def _():
            for g in range(relayed):
                forward(g).wait_send()

    for e in range(1, m):
        sq_copy(e, lax.rem(gi + m - e, m)).wait_recv()
    total = sqs[0]
    for e in range(1, m):
        total += sqs[e]
    scale = lax.rsqrt(jnp.sum(total, axis=0, keepdims=True) / D + 1e-06)
    scale = jnp.broadcast_to(scale, (GW, tokens)).T
    for g in range(groups):
        lane = slice(g * GW, (g + 1) * GW)
        out[:, lane] = (acc[g] * scale * gain[:, lane]).astype(BF16)

    for e in range(1, m):
        sq_copy(e, lax.rem(gi + e, m)).wait_send()


def on_device(n, m, q_in, k_in, v_in, fir, skip, taps, segments, gain):
    tokens, width = q_in.shape
    groups = width // GW
    far = n - 2
    vmem = pl.BlockSpec(memory_space=pltpu.VMEM)
    hbm = pl.BlockSpec(memory_space=pltpu.HBM)
    block = (groups, tokens, GW)
    dma = pltpu.SemaphoreType.DMA
    return pl.pallas_call(
        functools.partial(kernel, n, m, groups),
        out_shape=pltpu.VMEM((tokens, width), BF16),
        in_specs=[hbm] * 8,
        out_specs=vmem,
        scratch_shapes=[
            pltpu.VMEM((tokens, width), BF16),
            pltpu.VMEM((tokens, width), BF16),
            pltpu.VMEM((tokens, width), BF16),
            pltpu.VMEM(fir.shape, F32),
            pltpu.VMEM((1, width), F32),
            pltpu.VMEM(taps.shape, BF16),
            pltpu.VMEM((1, tokens), jnp.int32),
            pltpu.VMEM((1, width), F32),
            pltpu.VMEM(block, BF16),
            pltpu.VMEM((far,) + block, BF16),
            pltpu.VMEM((2, 16, width // 2), BF16),
            pltpu.VMEM((far + 1, 16, 2 * GW), BF16),
            pltpu.VMEM((far + 1,) + block, BF16),
            pltpu.VMEM((far + 1, tokens, GW), BF16),
            pltpu.VMEM(block, F32),
            pltpu.VMEM(block, F32),
            pltpu.VMEM((m, 8, tokens), F32),
            dma((8,)),
            dma((2,)),
            dma((far,)),
            dma((far,)),
            dma((far, groups)),
            dma((far, groups)),
            dma((groups,)),
            dma((m - 1,)),
            dma((m - 1,)),
        ],
        compiler_params=pltpu.CompilerParams(
            collective_id=0, has_side_effects=True, vmem_limit_bytes=40 * 1024 * 1024
        ),
        cost_estimate=pl.CostEstimate(
            flops=2 * tokens * tokens * width * (far + 1), bytes_accessed=8 * tokens * width, transcendentals=0
        ),
        name="mixer",
    )(*[
        pltpu.with_memory_space_constraint(x, pltpu.HBM)
        for x in (q_in, k_in, v_in, fir, skip[None, :], taps, segments[None, :], gain[None, :])
    ])


def solution(mesh):
    return jax.shard_map(
        functools.partial(on_device, mesh.shape["ctx"], mesh.shape["grp"]),
        mesh=mesh,
        in_specs=(
            P("ctx", "grp"),
            P("ctx", "grp"),
            P("ctx", "grp"),
            P(None, None, "grp"),
            P("grp"),
            P("grp", None),
            P("ctx"),
            P("grp"),
        ),
        out_specs=P("ctx", "grp"),
        check_vma=False,
    )
```

```python
import functools

import jax
import jax.numpy as jnp
from jax import lax
from jax.experimental import pallas as pl
from jax.experimental.pallas import tpu as pltpu
from jax.sharding import PartitionSpec as P

D = 8192
GW = 128
F32 = jnp.float32
BF16 = jnp.bfloat16
MESH = pl.DeviceIdType.MESH


def lagged(x, by, rows):
    return jnp.where(rows >= by, pltpu.roll(x, by, 0), 0.0)


def each(start, stop, step):
    def body(g, carry):
        step(g)
        return carry

    lax.fori_loop(start, stop, body, 0)


def lanes(g):
    return pl.ds(pl.multiple_of(g * GW, GW), GW)


def kernel(
    n, m, groups,
    q_hbm, k_hbm, v_hbm, fir_hbm, skip_hbm, taps_hbm, seg_hbm, gain_hbm, out,
    qbuf, kbuf, vbuf, fir, skip, taps, seg, gain, own, slots, halo, edges, fixes, before, backs, mats, masks, acc, fq, sqs,
    in_sem, halo_sem, edge_send, edge_recv, kv_send, kv_recv, fwd_send, sq_send, sq_recv,
):
    me, gi = lax.axis_index("ctx"), lax.axis_index("grp")
    tokens, width = qbuf.shape
    far = n - 2
    relay = n == 4
    relayed = groups - max(1, groups // 4) if relay else groups

    pairs = (
        (k_hbm, kbuf), (v_hbm, vbuf), (q_hbm, qbuf), (fir_hbm, fir),
        (seg_hbm, seg), (taps_hbm, taps), (skip_hbm, skip), (gain_hbm, gain),
    )
    loads = [pltpu.make_async_copy(src, dst, in_sem.at[i]) for i, (src, dst) in enumerate(pairs)]
    for load in loads:
        load.start()
    barrier = pltpu.get_barrier_semaphore()
    for d in range(1, n):
        pl.semaphore_signal(barrier, inc=1, device_id={"ctx": lax.rem(me + d, n)}, device_id_type=MESH)
    for e in range(1, m):
        pl.semaphore_signal(barrier, inc=1, device_id={"grp": lax.rem(gi + e, m)}, device_id_type=MESH)
    def halo_copy(peer):
        return pltpu.make_async_remote_copy(
            src_ref=halo.at[0], dst_ref=halo.at[1], send_sem=halo_sem.at[0], recv_sem=halo_sem.at[1],
            device_id={"ctx": peer}, device_id_type=MESH)

    def edge_copy(d, peer):
        return pltpu.make_async_remote_copy(
            src_ref=edges.at[0], dst_ref=edges.at[d], send_sem=edge_send.at[d - 1], recv_sem=edge_recv.at[d - 1],
            device_id={"ctx": peer}, device_id_type=MESH)

    def kv_copy(d, g, peer):
        return pltpu.make_async_remote_copy(
            src_ref=own.at[g], dst_ref=slots.at[d - 1, g], send_sem=kv_send.at[d - 1, g],
            recv_sem=kv_recv.at[d - 1, g], device_id={"ctx": peer}, device_id_type=MESH)

    def forward(g):
        return pltpu.make_async_remote_copy(
            src_ref=slots.at[1, g], dst_ref=slots.at[0, g], send_sem=fwd_send.at[g],
            recv_sem=kv_recv.at[0, g], device_id={"ctx": 2}, device_id_type=MESH)

    def sends(d):
        there = me + d < n
        return there & (me != 1) if relay and d == 1 else there

    def pass_on(g):
        if relay:
            @pl.when((me == 3) & (g < relayed))
            def _():
                kv_copy(2, g, 1).wait_recv()
                forward(g).start()

    rows = lax.broadcasted_iota(jnp.int32, (tokens, GW), 0)
    cols = lax.broadcasted_iota(jnp.int32, (tokens, GW), 1)
    row8 = lax.broadcasted_iota(jnp.int32, (8, width), 0)
    for load in loads:
        load.wait()

    def last8(ref, by):
        return pltpu.roll(ref[tokens - 16 :, :].astype(F32)[8:], by, 0)

    def first8(ref, by):
        return pltpu.roll(ref[:16, :].astype(F32)[:8], by, 0)

    half = width // 2
    last = jnp.where(row8 < 2, last8(kbuf, 2), jnp.where(row8 < 4, last8(qbuf, 4), last8(vbuf, 6)))
    halo[0] = jnp.concatenate([last[:, :half], last[:, half:]], axis=0).astype(BF16)

    def product(g):
        lane = lanes(g)

        def filtered(ref, a):
            x = ref[:, lane].astype(F32)
            return (fir[a, 0:1, lane] * x + fir[a, 1:2, lane] * lagged(x, 1, rows)
                    + fir[a, 2:3, lane] * lagged(x, 2, rows))

        own[g] = (filtered(kbuf, 1) * filtered(vbuf, 2)).astype(BF16)

    def send_chunk(g):
        for d in range(far, 0, -1):
            @pl.when(sends(d))
            def _():
                kv_copy(d, g, me + d).start()

    each(0, groups - relayed + 1, lambda i: product(lax.rem(i + relayed, groups)))
    pl.semaphore_wait(barrier, n - 1 + m - 1)
    @pl.when(me + 1 < n)
    def _():
        halo_copy(me + 1).start()

    if relay:
        @pl.when(me == 1)
        def _():
            for g in range(relayed, groups):
                kv_copy(1, g, 2).start()

    send_chunk(0)
    early = min(3, groups)

    def made_and_sent(g):
        @pl.when(g < relayed)
        def _():
            product(g)

        send_chunk(g)

    each(1, early, made_and_sent)

    @pl.when(me >= 1)
    def _():
        halo_copy(me - 1).wait_recv()

    came = halo[1].astype(F32)
    came = jnp.where(me >= 1, jnp.concatenate([came[:8], came[8:]], axis=1), 0.0)
    before[...] = came
    edge = jnp.where(
        lax.rem(row8, 4) < 2, came, jnp.where(row8 < 4, first8(kbuf, 2), first8(vbuf, 6)))
    tap = [jnp.where(row8 < 4, fir[1, i : i + 1, :], fir[2, i : i + 1, :]) for i in range(3)]
    both = tap[0] * edge + tap[1] * pltpu.roll(edge, 1, 0) + tap[2] * pltpu.roll(edge, 2, 0)
    fix = pltpu.roll(both * pltpu.roll(both, 4, 0), 6, 0)
    small8 = row8[:, :GW]
    folded = [jnp.zeros((8, GW), F32)] * 2
    for g in range(groups):
        t, j = g // 4, 2 * (g % 4)
        piece = fix[:, g * GW : (g + 1) * GW]
        fixes[0, g] = piece
        piece = pltpu.roll(piece, j, 0) if j else piece
        folded[t] = jnp.where((small8 >= j) & (small8 < j + 2), piece, folded[t])
    seg_f = seg[...].astype(F32)
    edges[0] = jnp.concatenate(
        [jnp.concatenate(folded, axis=0), jnp.broadcast_to(seg_f, (16, GW))], axis=1).astype(BF16)
    for d in range(1, far + 1):
        @pl.when(me + d < n)
        def _():
            edge_copy(d, me + d).start()
    passed = early + 2

    def late(g):
        made_and_sent(g)

        @pl.when(g >= passed)
        def _():
            pass_on(g - passed)

    each(early, groups, late)
    passed = max(0, groups - passed)

    def block_of(ref, d, g):
        first = fixes[d, g]
        whole = ref[...]
        top = whole[:16].astype(F32)
        head = jnp.concatenate([jnp.where(small8 < 2, first, top[:8]), top[8:]], axis=0)
        return jnp.concatenate([head.astype(BF16), whole[16:]], axis=0)

    flip = (rows + cols == GW - 1).astype(BF16)
    target = jnp.broadcast_to(seg_f, (tokens, GW)).T

    def mask(d):
        return jnp.where(edges[d].astype(F32)[:1, GW:] == target, 1.0, 0.0).astype(BF16)

    masks[0] = mask(0)
    for d in range(far + 1):
        backs[d] = jnp.dot(taps[:, d * GW : (d + 1) * GW], flip, preferred_element_type=F32)

    def prepare(g):
        lane = lanes(g)
        nearer = 0.0
        for d in range(far + 1):
            back = jnp.broadcast_to(backs[d, pl.ds(g, 1), :], (tokens, GW))
            turned = pltpu.roll(back, 1, 1, stride=1, stride_axis=0)
            mats[d, g] = jnp.where(cols <= rows, turned, nearer).astype(BF16)
            nearer = turned
        block = block_of(own.at[g], 0, g)
        acc[g] = (jnp.dot(mats[0, g] * masks[0], block, preferred_element_type=F32)
                  + skip[:, lane] * block.astype(F32))
        x = qbuf[:, lane].astype(F32)
        last2, last1 = before[2:3, lane], before[3:4, lane]
        one = jnp.where(rows < 1, last1, pltpu.roll(x, 1, 0))
        two = jnp.where(rows < 1, last2, jnp.where(rows < 2, last1, pltpu.roll(x, 2, 0)))
        fq[g] = fir[0, 0:1, lane] * x + fir[0, 1:2, lane] * one + fir[0, 2:3, lane] * two

        @pl.when(lax.rem(g, 3) == 1)
        def _():
            pass_on(passed + g // 3)

    each(0, groups, prepare)
    done = passed + (groups + 1) // 3

    for d in range(1, far + 1):
        @pl.when(me >= d)
        def _():
            edge_copy(d, me - d).wait_recv()
            masks[d] = mask(d)
            found = edges[d].astype(F32)
            for g in range(groups):
                t, j = g // 4, 2 * (g % 4)
                first = found[8 * t : 8 * t + 8, :GW]
                fixes[d, g] = pltpu.roll(first, 8 - j, 0) if j else first

    def receive(g, squares):
        if done < relayed:
            pass_on(done + g)
        for d in range(far, 0, -1):
            @pl.when(me >= d)
            def _():
                if relay and d == 2:
                    @pl.when((me == 2) | (g >= relayed))
                    def _():
                        kv_copy(d, g, me - d).wait_recv()
                else:
                    kv_copy(d, g, me - d).wait_recv()
                acc[g] += jnp.dot(
                    mats[d, g] * masks[d], block_of(slots.at[d - 1, g], d, g), preferred_element_type=F32)
        gated = fq[g] * acc[g]
        acc[g] = gated
        return squares + gated * gated

    squares = lax.fori_loop(0, groups, receive, jnp.zeros((tokens, GW), F32))
    sqs[0] = jnp.sum(squares.T.reshape(GW // 8, 8, tokens), axis=0)

    def sq_copy(e, peer):
        return pltpu.make_async_remote_copy(
            src_ref=sqs.at[0], dst_ref=sqs.at[e], send_sem=sq_send.at[e - 1], recv_sem=sq_recv.at[e - 1],
            device_id={"grp": peer}, device_id_type=MESH)

    for e in range(1, m):
        sq_copy(e, lax.rem(gi + e, m)).start()

    @pl.when(me + 1 < n)
    def _():
        halo_copy(me + 1).wait_send()

    for d in range(1, far + 1):
        @pl.when(me + d < n)
        def _():
            edge_copy(d, me + d).wait_send()
    for d in range(1, far + 1):
        for g in range(groups):
            @pl.when(sends(d))
            def _():
                kv_copy(d, g, me + d).wait_send()
    if relay:
        @pl.when(me == 1)
        def _():
            for g in range(relayed, groups):
                kv_copy(1, g, 2).wait_send()

        @pl.when(me == 3)
        def _():
            for g in range(relayed):
                forward(g).wait_send()

    for e in range(1, m):
        sq_copy(e, lax.rem(gi + m - e, m)).wait_recv()
    total = sqs[0]
    for e in range(1, m):
        total += sqs[e]
    scale = lax.rsqrt(jnp.sum(total, axis=0, keepdims=True) / D + 1e-06)
    scale = jnp.broadcast_to(scale, (GW, tokens)).T

    def finish(g):
        lane = lanes(g)
        out[:, lane] = (acc[g] * scale * gain[:, lane]).astype(BF16)

    each(0, groups, finish)

    for e in range(1, m):
        sq_copy(e, lax.rem(gi + e, m)).wait_send()


def on_device(n, m, q_in, k_in, v_in, fir, skip, taps, segments, gain):
    tokens, width = q_in.shape
    groups = width // GW
    far = n - 2
    vmem = pl.BlockSpec(memory_space=pltpu.VMEM)
    hbm = pl.BlockSpec(memory_space=pltpu.HBM)
    block = (groups, tokens, GW)
    dma = pltpu.SemaphoreType.DMA
    return pl.pallas_call(
        functools.partial(kernel, n, m, groups),
        out_shape=pltpu.VMEM((tokens, width), BF16),
        in_specs=[hbm] * 8,
        out_specs=vmem,
        scratch_shapes=[
            pltpu.VMEM((tokens, width), BF16),
            pltpu.VMEM((tokens, width), BF16),
            pltpu.VMEM((tokens, width), BF16),
            pltpu.VMEM(fir.shape, F32),
            pltpu.VMEM((1, width), F32),
            pltpu.VMEM(taps.shape, BF16),
            pltpu.VMEM((1, tokens), jnp.int32),
            pltpu.VMEM((1, width), F32),
            pltpu.VMEM(block, BF16),
            pltpu.VMEM((far,) + block, BF16),
            pltpu.VMEM((2, 16, width // 2), BF16),
            pltpu.VMEM((far + 1, 16, 2 * GW), BF16),
            pltpu.VMEM((far + 1, groups, 8, GW), F32),
            pltpu.VMEM((8, width), F32),
            pltpu.VMEM((far + 1, groups, GW), F32),
            pltpu.VMEM((far + 1,) + block, BF16),
            pltpu.VMEM((far + 1, tokens, GW), BF16),
            pltpu.VMEM(block, F32),
            pltpu.VMEM(block, F32),
            pltpu.VMEM((m, 8, tokens), F32),
            dma((8,)),
            dma((2,)),
            dma((far,)),
            dma((far,)),
            dma((far, groups)),
            dma((far, groups)),
            dma((groups,)),
            dma((m - 1,)),
            dma((m - 1,)),
        ],
        compiler_params=pltpu.CompilerParams(
            collective_id=0, has_side_effects=True, vmem_limit_bytes=40 * 1024 * 1024
        ),
        cost_estimate=pl.CostEstimate(
            flops=2 * tokens * tokens * width * (far + 1), bytes_accessed=8 * tokens * width, transcendentals=0
        ),
        name="mixer",
    )(*[
        pltpu.with_memory_space_constraint(x, pltpu.HBM)
        for x in (q_in, k_in, v_in, fir, skip[None, :], taps, segments[None, :], gain[None, :])
    ])


def solution(mesh):
    return jax.shard_map(
        functools.partial(on_device, mesh.shape["ctx"], mesh.shape["grp"]),
        mesh=mesh,
        in_specs=(
            P("ctx", "grp"),
            P("ctx", "grp"),
            P("ctx", "grp"),
            P(None, None, "grp"),
            P("grp"),
            P("grp", None),
            P("ctx"),
            P("grp"),
        ),
        out_specs=P("ctx", "grp"),
        check_vma=False,
    )
```

```python
import functools

import jax
import jax.numpy as jnp
from jax import lax
from jax.experimental import pallas as pl
from jax.experimental.pallas import tpu as pltpu
from jax.sharding import PartitionSpec as P

D = 8192
GW = 128
F32 = jnp.float32
BF16 = jnp.bfloat16
MESH = pl.DeviceIdType.MESH


def lagged(x, by, rows):
    return jnp.where(rows >= by, pltpu.roll(x, by, 0), 0.0)


def kernel(
    n, m, groups,
    q_hbm, k_hbm, v_hbm, fir_hbm, skip_hbm, taps_hbm, seg_hbm, gain_hbm, out,
    qbuf, kbuf, vbuf, fir, skip, taps, seg, gain, own, slots, halo, edges, mats, masks, acc, fq, sqs,
    in_sem, halo_sem, edge_send, edge_recv, kv_send, kv_recv, fwd_send, sq_send, sq_recv,
):
    me, gi = lax.axis_index("ctx"), lax.axis_index("grp")
    tokens, width = qbuf.shape
    far = n - 2
    relay = n == 4
    relayed = groups - max(1, groups // 4)

    pairs = (
        (k_hbm, kbuf), (v_hbm, vbuf), (q_hbm, qbuf), (fir_hbm, fir),
        (seg_hbm, seg), (taps_hbm, taps), (skip_hbm, skip), (gain_hbm, gain),
    )
    loads = [pltpu.make_async_copy(src, dst, in_sem.at[i]) for i, (src, dst) in enumerate(pairs)]
    for load in loads:
        load.start()
    barrier = pltpu.get_barrier_semaphore()
    for d in range(1, n):
        pl.semaphore_signal(barrier, inc=1, device_id={"ctx": lax.rem(me + d, n)}, device_id_type=MESH)
    for e in range(1, m):
        pl.semaphore_signal(barrier, inc=1, device_id={"grp": lax.rem(gi + e, m)}, device_id_type=MESH)
    def halo_copy(peer):
        return pltpu.make_async_remote_copy(
            src_ref=halo.at[0], dst_ref=halo.at[1], send_sem=halo_sem.at[0], recv_sem=halo_sem.at[1],
            device_id={"ctx": peer}, device_id_type=MESH)

    def edge_copy(d, peer):
        return pltpu.make_async_remote_copy(
            src_ref=edges.at[0], dst_ref=edges.at[d], send_sem=edge_send.at[d - 1], recv_sem=edge_recv.at[d - 1],
            device_id={"ctx": peer}, device_id_type=MESH)

    def kv_copy(d, g, peer):
        return pltpu.make_async_remote_copy(
            src_ref=own.at[g], dst_ref=slots.at[d - 1, g], send_sem=kv_send.at[d - 1, g],
            recv_sem=kv_recv.at[d - 1, g], device_id={"ctx": peer}, device_id_type=MESH)

    def forward(g):
        return pltpu.make_async_remote_copy(
            src_ref=slots.at[1, g], dst_ref=slots.at[0, g], send_sem=fwd_send.at[g],
            recv_sem=kv_recv.at[0, g], device_id={"ctx": 2}, device_id_type=MESH)

    def sends(d, g):
        there = me + d < n
        return there & (me != 1) if relay and d == 1 else there

    def pass_on(g):
        if relay and g < relayed:
            @pl.when(me == 3)
            def _():
                kv_copy(2, g, 1).wait_recv()
                forward(g).start()

    rows = lax.broadcasted_iota(jnp.int32, (tokens, GW), 0)
    cols = lax.broadcasted_iota(jnp.int32, (tokens, GW), 1)
    row8 = lax.broadcasted_iota(jnp.int32, (8, width), 0)
    for load in loads:
        load.wait()

    def last8(ref, by):
        return pltpu.roll(ref[tokens - 16 :, :].astype(F32)[8:], by, 0)

    def first8(ref, by):
        return pltpu.roll(ref[:16, :].astype(F32)[:8], by, 0)

    half = width // 2
    last = jnp.where(row8 < 2, last8(kbuf, 2), jnp.where(row8 < 4, last8(qbuf, 4), last8(vbuf, 6)))
    halo[0] = jnp.concatenate([last[:, :half], last[:, half:]], axis=0).astype(BF16)

    def product(g):
        lane = slice(g * GW, (g + 1) * GW)

        def filtered(ref, a):
            x = ref[:, lane].astype(F32)
            return (fir[a, 0:1, lane] * x + fir[a, 1:2, lane] * lagged(x, 1, rows)
                    + fir[a, 2:3, lane] * lagged(x, 2, rows))

        own[g] = (filtered(kbuf, 1) * filtered(vbuf, 2)).astype(BF16)

    def send_chunk(g):
        for d in range(far, 0, -1):
            @pl.when(sends(d, g))
            def _():
                kv_copy(d, g, me + d).start()

    direct = range(relayed, groups) if relay else range(0)
    for g in (*direct, 0):
        product(g)
    pl.semaphore_wait(barrier, n - 1 + m - 1)
    @pl.when(me + 1 < n)
    def _():
        halo_copy(me + 1).start()

    if relay:
        @pl.when(me == 1)
        def _():
            for g in direct:
                kv_copy(1, g, 2).start()

    send_chunk(0)
    early = min(3, groups)
    for g in range(1, early):
        product(g)
        send_chunk(g)

    @pl.when(me >= 1)
    def _():
        halo_copy(me - 1).wait_recv()

    before = halo[1].astype(F32)
    before = jnp.where(me >= 1, jnp.concatenate([before[:8], before[8:]], axis=1), 0.0)
    edge = jnp.where(
        lax.rem(row8, 4) < 2, before, jnp.where(row8 < 4, first8(kbuf, 2), first8(vbuf, 6)))
    tap = [jnp.where(row8 < 4, fir[1, i : i + 1, :], fir[2, i : i + 1, :]) for i in range(3)]
    both = tap[0] * edge + tap[1] * pltpu.roll(edge, 1, 0) + tap[2] * pltpu.roll(edge, 2, 0)
    fix = pltpu.roll(both * pltpu.roll(both, 4, 0), 6, 0)
    small8 = row8[:, :GW]
    folded = [jnp.zeros((8, GW), F32)] * 2
    for g in range(groups):
        t, j = g // 4, 2 * (g % 4)
        piece = fix[:, g * GW : (g + 1) * GW]
        piece = pltpu.roll(piece, j, 0) if j else piece
        folded[t] = jnp.where((small8 >= j) & (small8 < j + 2), piece, folded[t])
    seg_f = seg[...].astype(F32)
    edges[0] = jnp.concatenate(
        [jnp.concatenate(folded, axis=0), jnp.broadcast_to(seg_f, (16, GW))], axis=1).astype(BF16)
    for d in range(1, far + 1):
        @pl.when(me + d < n)
        def _():
            edge_copy(d, me + d).start()
    passed = 0
    for g in range(early, groups):
        if g not in direct:
            product(g)
        send_chunk(g)
        if g >= early + 2:
            pass_on(passed)
            passed += 1

    def block_of(ref, d, g):
        t, j = g // 4, 2 * (g % 4)
        first = edges[d].astype(F32)[8 * t : 8 * t + 8, :GW]
        first = pltpu.roll(first, 8 - j, 0) if j else first
        whole = ref[...]
        top = whole[:16].astype(F32)
        head = jnp.concatenate([jnp.where(small8 < 2, first, top[:8]), top[8:]], axis=0)
        return jnp.concatenate([head.astype(BF16), whole[16:]], axis=0)

    flip = (rows + cols == GW - 1).astype(BF16)
    target = jnp.broadcast_to(seg_f, (tokens, GW)).T

    def mask(d):
        return jnp.where(edges[d].astype(F32)[:1, GW:] == target, 1.0, 0.0).astype(BF16)

    masks[0] = mask(0)
    back = [
        jnp.dot(taps[:, d * GW : (d + 1) * GW], flip, preferred_element_type=F32) for d in range(far + 1)
    ]
    for g in range(groups):
        lane = slice(g * GW, (g + 1) * GW)
        nearer = 0.0
        for d in range(far + 1):
            turned = pltpu.roll(jnp.broadcast_to(back[d][g : g + 1], (tokens, GW)), 1, 1, stride=1, stride_axis=0)
            mats[d, g] = jnp.where(cols <= rows, turned, nearer).astype(BF16)
            nearer = turned
        block = block_of(own.at[g], 0, g)
        acc[g] = (jnp.dot(mats[0, g] * masks[0], block, preferred_element_type=F32)
                  + skip[:, lane] * block.astype(F32))
        x = qbuf[:, lane].astype(F32)
        one = jnp.where(rows < 1, before[3:4, lane], pltpu.roll(x, 1, 0))
        two = jnp.where(rows < 1, before[2:3, lane], jnp.where(rows < 2, before[3:4, lane], pltpu.roll(x, 2, 0)))
        fq[g] = fir[0, 0:1, lane] * x + fir[0, 1:2, lane] * one + fir[0, 2:3, lane] * two
        if g % 3 == 1:
            pass_on(passed)
            passed += 1

    for d in range(1, far + 1):
        @pl.when(me >= d)
        def _():
            edge_copy(d, me - d).wait_recv()
            masks[d] = mask(d)

    def receive(d, g):
        if relay and d == 2 and g < relayed:
            @pl.when(me == 2)
            def _():
                kv_copy(d, g, me - d).wait_recv()
        else:
            kv_copy(d, g, me - d).wait_recv()

    def add_blocks(pair, sources):
        for g in pair:
            for d in sources:
                receive(d, g)
        for g in pair:
            left = jnp.concatenate([mats[d, g] * masks[d] for d in sources], axis=1)
            right = jnp.concatenate([block_of(slots.at[d - 1, g], d, g) for d in sources], axis=0)
            acc[g] += jnp.dot(left, right, preferred_element_type=F32)

    squares = jnp.zeros((tokens, GW), F32)
    for start in range(0, groups, 2):
        pair = range(start, min(start + 2, groups))
        for g in pair:
            pass_on(passed)
            passed += 1
        if relay:
            pl.when(me == 1)(functools.partial(add_blocks, pair, (1,)))
            pl.when(me >= 2)(functools.partial(add_blocks, pair, (2, 1)))
        else:
            for d in range(far, 0, -1):
                pl.when(me >= d)(functools.partial(add_blocks, pair, (d,)))
        for g in pair:
            gated = fq[g] * acc[g]
            acc[g] = gated
            squares += gated * gated

    sqs[0] = jnp.sum(squares.T, axis=0, keepdims=True)

    if m == 8:
        z, core = lax.div(gi, 2), lax.rem(gi, 2)
        chips = (3 - z, lax.rem(z + 2, 4), z + 1 - 2 * lax.rem(z, 2))
        peers = [2 * chip + c for chip in chips for c in (core, 1 - core)] + [2 * z + 1 - core]
        sources = peers
    else:
        peers = [lax.rem(gi + e, m) for e in range(1, m)]
        sources = [lax.rem(gi + m - e, m) for e in range(1, m)]

    def sq_copy(e, peer):
        return pltpu.make_async_remote_copy(
            src_ref=sqs.at[0], dst_ref=sqs.at[e], send_sem=sq_send.at[e - 1], recv_sem=sq_recv.at[e - 1],
            device_id={"grp": peer}, device_id_type=MESH)

    for e in range(1, m):
        sq_copy(e, peers[e - 1]).start()

    @pl.when(me + 1 < n)
    def _():
        halo_copy(me + 1).wait_send()

    for d in range(1, far + 1):
        @pl.when(me + d < n)
        def _():
            edge_copy(d, me + d).wait_send()
    for d in range(1, far + 1):
        for g in range(groups):
            @pl.when(sends(d, g))
            def _():
                kv_copy(d, g, me + d).wait_send()
    if relay:
        @pl.when(me == 1)
        def _():
            for g in direct:
                kv_copy(1, g, 2).wait_send()

        @pl.when(me == 3)
        def _():
            for g in range(relayed):
                forward(g).wait_send()

    for e in range(1, m):
        sq_copy(e, sources[e - 1]).wait_recv()
    total = sqs[0]
    for e in range(1, m):
        total += sqs[e]
    scale = lax.rsqrt(total / D + 1e-06)
    scale = jnp.broadcast_to(scale, (GW, tokens)).T
    for g in range(groups):
        lane = slice(g * GW, (g + 1) * GW)
        out[:, lane] = (acc[g] * scale * gain[:, lane]).astype(BF16)

    for e in range(1, m):
        sq_copy(e, peers[e - 1]).wait_send()


def on_device(n, m, q_in, k_in, v_in, fir, skip, taps, segments, gain):
    tokens, width = q_in.shape
    groups = width // GW
    far = n - 2
    vmem = pl.BlockSpec(memory_space=pltpu.VMEM)
    hbm = pl.BlockSpec(memory_space=pltpu.HBM)
    block = (groups, tokens, GW)
    dma = pltpu.SemaphoreType.DMA
    return pl.pallas_call(
        functools.partial(kernel, n, m, groups),
        out_shape=pltpu.VMEM((tokens, width), BF16),
        in_specs=[hbm] * 8,
        out_specs=vmem,
        scratch_shapes=[
            pltpu.VMEM((tokens, width), BF16),
            pltpu.VMEM((tokens, width), BF16),
            pltpu.VMEM((tokens, width), BF16),
            pltpu.VMEM(fir.shape, F32),
            pltpu.VMEM((1, width), F32),
            pltpu.VMEM(taps.shape, BF16),
            pltpu.VMEM((1, tokens), jnp.int32),
            pltpu.VMEM((1, width), F32),
            pltpu.VMEM(block, BF16),
            pltpu.VMEM((far,) + block, BF16),
            pltpu.VMEM((2, 16, width // 2), BF16),
            pltpu.VMEM((far + 1, 16, 2 * GW), BF16),
            pltpu.VMEM((far + 1,) + block, BF16),
            pltpu.VMEM((far + 1, tokens, GW), BF16),
            pltpu.VMEM(block, F32),
            pltpu.VMEM(block, F32),
            pltpu.VMEM((m, 1, tokens), F32),
            dma((8,)),
            dma((2,)),
            dma((far,)),
            dma((far,)),
            dma((far, groups)),
            dma((far, groups)),
            dma((groups,)),
            dma((m - 1,)),
            dma((m - 1,)),
        ],
        compiler_params=pltpu.CompilerParams(
            collective_id=0, has_side_effects=True, vmem_limit_bytes=40 * 1024 * 1024
        ),
        cost_estimate=pl.CostEstimate(
            flops=2 * tokens * tokens * width * (far + 1), bytes_accessed=8 * tokens * width, transcendentals=0
        ),
        name="mixer",
    )(*[
        pltpu.with_memory_space_constraint(x, pltpu.HBM)
        for x in (q_in, k_in, v_in, fir, skip[None, :], taps, segments[None, :], gain[None, :])
    ])


def solution(mesh):
    return jax.shard_map(
        functools.partial(on_device, mesh.shape["ctx"], mesh.shape["grp"]),
        mesh=mesh,
        in_specs=(
            P("ctx", "grp"),
            P("ctx", "grp"),
            P("ctx", "grp"),
            P(None, None, "grp"),
            P("grp"),
            P("grp", None),
            P("ctx"),
            P("grp"),
        ),
        out_specs=P("ctx", "grp"),
        check_vma=False,
    )
```

```python
import functools

import jax
import jax.numpy as jnp
from jax import lax
from jax.experimental import pallas as pl
from jax.experimental.pallas import tpu as pltpu
from jax.sharding import PartitionSpec as P

D = 8192
GW = 128
F32 = jnp.float32
BF16 = jnp.bfloat16
MESH = pl.DeviceIdType.MESH


def lagged(x, by, rows):
    return jnp.where(rows >= by, pltpu.roll(x, by, 0), 0.0)


def kernel(
    n, m, groups,
    q_hbm, k_hbm, v_hbm, fir_hbm, skip_hbm, taps_hbm, seg_hbm, gain_hbm, out,
    qbuf, kbuf, vbuf, fir, skip, taps, seg, gain, own, slots, halo, edges, mats, masks, acc, fq, sqs,
    in_sem, halo_sem, edge_send, edge_recv, kv_send, kv_recv, fwd_send, sq_send, sq_recv,
):
    me, gi = lax.axis_index("ctx"), lax.axis_index("grp")
    tokens, width = qbuf.shape
    far = n - 2
    relay = n == 4
    relayed = groups - max(1, groups // 8)

    pairs = (
        (k_hbm, kbuf), (v_hbm, vbuf), (q_hbm, qbuf), (fir_hbm, fir),
        (seg_hbm, seg), (taps_hbm, taps), (skip_hbm, skip), (gain_hbm, gain),
    )
    loads = [pltpu.make_async_copy(src, dst, in_sem.at[i]) for i, (src, dst) in enumerate(pairs)]
    for load in loads:
        load.start()
    barrier = pltpu.get_barrier_semaphore()
    for d in range(1, n):
        pl.semaphore_signal(barrier, inc=1, device_id={"ctx": lax.rem(me + d, n)}, device_id_type=MESH)
    for e in range(1, m):
        pl.semaphore_signal(barrier, inc=1, device_id={"grp": lax.rem(gi + e, m)}, device_id_type=MESH)
    def halo_copy(peer):
        return pltpu.make_async_remote_copy(
            src_ref=halo.at[0], dst_ref=halo.at[1], send_sem=halo_sem.at[0], recv_sem=halo_sem.at[1],
            device_id={"ctx": peer}, device_id_type=MESH)

    def edge_copy(d, peer):
        return pltpu.make_async_remote_copy(
            src_ref=edges.at[0], dst_ref=edges.at[d], send_sem=edge_send.at[d - 1], recv_sem=edge_recv.at[d - 1],
            device_id={"ctx": peer}, device_id_type=MESH)

    def kv_copy(d, g, peer):
        return pltpu.make_async_remote_copy(
            src_ref=own.at[g], dst_ref=slots.at[d - 1, g], send_sem=kv_send.at[d - 1, g],
            recv_sem=kv_recv.at[d - 1, g], device_id={"ctx": peer}, device_id_type=MESH)

    def forward(g):
        return pltpu.make_async_remote_copy(
            src_ref=slots.at[1, g], dst_ref=slots.at[0, g], send_sem=fwd_send.at[g],
            recv_sem=kv_recv.at[0, g], device_id={"ctx": 2}, device_id_type=MESH)

    def sends(d, g):
        there = me + d < n
        return there & (me != 1) if relay and d == 1 else there

    def pass_on(g):
        if relay and g < relayed:
            @pl.when(me == 3)
            def _():
                kv_copy(2, g, 1).wait_recv()
                forward(g).start()

    rows = lax.broadcasted_iota(jnp.int32, (tokens, GW), 0)
    cols = lax.broadcasted_iota(jnp.int32, (tokens, GW), 1)
    row8 = lax.broadcasted_iota(jnp.int32, (8, width), 0)
    for load in loads:
        load.wait()

    def last8(ref, by):
        return pltpu.roll(ref[tokens - 16 :, :].astype(F32)[8:], by, 0)

    def first8(ref, by):
        return pltpu.roll(ref[:16, :].astype(F32)[:8], by, 0)

    half = width // 2
    last = jnp.where(row8 < 2, last8(kbuf, 2), jnp.where(row8 < 4, last8(qbuf, 4), last8(vbuf, 6)))
    halo[0] = jnp.concatenate([last[:, :half], last[:, half:]], axis=0).astype(BF16)

    def product(g):
        lane = slice(g * GW, (g + 1) * GW)

        def filtered(ref, a):
            x = ref[:, lane].astype(F32)
            return (fir[a, 0:1, lane] * x + fir[a, 1:2, lane] * lagged(x, 1, rows)
                    + fir[a, 2:3, lane] * lagged(x, 2, rows))

        own[g] = (filtered(kbuf, 1) * filtered(vbuf, 2)).astype(BF16)

    def send_chunk(g):
        for d in range(far, 0, -1):
            @pl.when(sends(d, g))
            def _():
                kv_copy(d, g, me + d).start()

    direct = range(relayed, groups) if relay else range(0)
    for g in (*direct, 0):
        product(g)
    pl.semaphore_wait(barrier, n - 1 + m - 1)
    @pl.when(me + 1 < n)
    def _():
        halo_copy(me + 1).start()

    if relay:
        @pl.when(me == 1)
        def _():
            for g in direct:
                kv_copy(1, g, 2).start()

    send_chunk(0)
    early = min(3, groups)
    for g in range(1, early):
        product(g)
        send_chunk(g)

    @pl.when(me >= 1)
    def _():
        halo_copy(me - 1).wait_recv()

    before = halo[1].astype(F32)
    before = jnp.where(me >= 1, jnp.concatenate([before[:8], before[8:]], axis=1), 0.0)
    edge = jnp.where(
        lax.rem(row8, 4) < 2, before, jnp.where(row8 < 4, first8(kbuf, 2), first8(vbuf, 6)))
    tap = [jnp.where(row8 < 4, fir[1, i : i + 1, :], fir[2, i : i + 1, :]) for i in range(3)]
    both = tap[0] * edge + tap[1] * pltpu.roll(edge, 1, 0) + tap[2] * pltpu.roll(edge, 2, 0)
    fix = pltpu.roll(both * pltpu.roll(both, 4, 0), 6, 0)
    small8 = row8[:, :GW]
    folded = [jnp.zeros((8, GW), F32)] * 2
    for g in range(groups):
        t, j = g // 4, 2 * (g % 4)
        piece = fix[:, g * GW : (g + 1) * GW]
        piece = pltpu.roll(piece, j, 0) if j else piece
        folded[t] = jnp.where((small8 >= j) & (small8 < j + 2), piece, folded[t])
    seg_f = seg[...].astype(F32)
    edges[0] = jnp.concatenate(
        [jnp.concatenate(folded, axis=0), jnp.broadcast_to(seg_f, (16, GW))], axis=1).astype(BF16)
    for d in range(1, far + 1):
        @pl.when(me + d < n)
        def _():
            edge_copy(d, me + d).start()
    passed = 0
    for g in range(early, groups):
        if g not in direct:
            product(g)
        send_chunk(g)
        if g >= early + 2:
            pass_on(passed)
            passed += 1

    def block_of(ref, d, g):
        t, j = g // 4, 2 * (g % 4)
        first = edges[d].astype(F32)[8 * t : 8 * t + 8, :GW]
        first = pltpu.roll(first, 8 - j, 0) if j else first
        whole = ref[...]
        top = whole[:16].astype(F32)
        head = jnp.concatenate([jnp.where(small8 < 2, first, top[:8]), top[8:]], axis=0)
        return jnp.concatenate([head.astype(BF16), whole[16:]], axis=0)

    flip = (rows + cols == GW - 1).astype(BF16)
    target = jnp.broadcast_to(seg_f, (tokens, GW)).T

    def mask(d):
        return jnp.where(edges[d].astype(F32)[:1, GW:] == target, 1.0, 0.0).astype(BF16)

    masks[0] = mask(0)
    back = [
        jnp.dot(taps[:, d * GW : (d + 1) * GW], flip, preferred_element_type=F32) for d in range(far + 1)
    ]
    for g in range(groups):
        lane = slice(g * GW, (g + 1) * GW)
        nearer = 0.0
        for d in range(far + 1):
            turned = pltpu.roll(jnp.broadcast_to(back[d][g : g + 1], (tokens, GW)), 1, 1, stride=1, stride_axis=0)
            mats[d, g] = jnp.where(cols <= rows, turned, nearer).astype(BF16)
            nearer = turned
        block = block_of(own.at[g], 0, g)
        acc[g] = (jnp.dot(mats[0, g] * masks[0], block, preferred_element_type=F32)
                  + skip[:, lane] * block.astype(F32))
        x = qbuf[:, lane].astype(F32)
        one = jnp.where(rows < 1, before[3:4, lane], pltpu.roll(x, 1, 0))
        two = jnp.where(rows < 1, before[2:3, lane], jnp.where(rows < 2, before[3:4, lane], pltpu.roll(x, 2, 0)))
        fq[g] = fir[0, 0:1, lane] * x + fir[0, 1:2, lane] * one + fir[0, 2:3, lane] * two
        if g % 3 == 1:
            pass_on(passed)
            passed += 1

    for d in range(1, far + 1):
        @pl.when(me >= d)
        def _():
            edge_copy(d, me - d).wait_recv()
            masks[d] = mask(d)

    def receive(d, g):
        if relay and d == 2 and g < relayed:
            @pl.when(me == 2)
            def _():
                kv_copy(d, g, me - d).wait_recv()
        else:
            kv_copy(d, g, me - d).wait_recv()

    def add_blocks(pair, sources):
        for g in pair:
            for d in sources:
                receive(d, g)
        for g in pair:
            left = jnp.concatenate([mats[d, g] * masks[d] for d in sources], axis=1)
            right = jnp.concatenate([block_of(slots.at[d - 1, g], d, g) for d in sources], axis=0)
            acc[g] += jnp.dot(left, right, preferred_element_type=F32)

    squares = jnp.zeros((tokens, GW), F32)
    for start in range(0, groups, 2):
        pair = range(start, min(start + 2, groups))
        for g in pair:
            pass_on(passed)
            passed += 1
        if relay:
            pl.when(me == 1)(functools.partial(add_blocks, pair, (1,)))
            pl.when(me >= 2)(functools.partial(add_blocks, pair, (2, 1)))
        else:
            for d in range(far, 0, -1):
                pl.when(me >= d)(functools.partial(add_blocks, pair, (d,)))
        for g in pair:
            gated = fq[g] * acc[g]
            acc[g] = gated
            squares += gated * gated

    sqs[0] = jnp.sum(squares.T, axis=0, keepdims=True)

    if m == 8:
        z, core = lax.div(gi, 2), lax.rem(gi, 2)
        chips = (3 - z, lax.rem(z + 2, 4), z + 1 - 2 * lax.rem(z, 2))
        peers = [2 * chip + c for chip in chips for c in (core, 1 - core)] + [2 * z + 1 - core]
        sources = peers
    else:
        peers = [lax.rem(gi + e, m) for e in range(1, m)]
        sources = [lax.rem(gi + m - e, m) for e in range(1, m)]

    def sq_copy(e, peer):
        return pltpu.make_async_remote_copy(
            src_ref=sqs.at[0], dst_ref=sqs.at[e], send_sem=sq_send.at[e - 1], recv_sem=sq_recv.at[e - 1],
            device_id={"grp": peer}, device_id_type=MESH)

    for e in range(1, m):
        sq_copy(e, peers[e - 1]).start()

    @pl.when(me + 1 < n)
    def _():
        halo_copy(me + 1).wait_send()

    for d in range(1, far + 1):
        @pl.when(me + d < n)
        def _():
            edge_copy(d, me + d).wait_send()
    for d in range(1, far + 1):
        for g in range(groups):
            @pl.when(sends(d, g))
            def _():
                kv_copy(d, g, me + d).wait_send()
    if relay:
        @pl.when(me == 1)
        def _():
            for g in direct:
                kv_copy(1, g, 2).wait_send()

        @pl.when(me == 3)
        def _():
            for g in range(relayed):
                forward(g).wait_send()

    for e in range(1, m):
        sq_copy(e, sources[e - 1]).wait_recv()
    total = sqs[0]
    for e in range(1, m):
        total += sqs[e]
    scale = lax.rsqrt(total / D + 1e-06)
    scale = jnp.broadcast_to(scale, (GW, tokens)).T
    for g in range(groups):
        lane = slice(g * GW, (g + 1) * GW)
        out[:, lane] = (acc[g] * scale * gain[:, lane]).astype(BF16)

    for e in range(1, m):
        sq_copy(e, peers[e - 1]).wait_send()


def on_device(n, m, q_in, k_in, v_in, fir, skip, taps, segments, gain):
    tokens, width = q_in.shape
    groups = width // GW
    far = n - 2
    vmem = pl.BlockSpec(memory_space=pltpu.VMEM)
    hbm = pl.BlockSpec(memory_space=pltpu.HBM)
    block = (groups, tokens, GW)
    dma = pltpu.SemaphoreType.DMA
    return pl.pallas_call(
        functools.partial(kernel, n, m, groups),
        out_shape=pltpu.VMEM((tokens, width), BF16),
        in_specs=[hbm] * 8,
        out_specs=vmem,
        scratch_shapes=[
            pltpu.VMEM((tokens, width), BF16),
            pltpu.VMEM((tokens, width), BF16),
            pltpu.VMEM((tokens, width), BF16),
            pltpu.VMEM(fir.shape, F32),
            pltpu.VMEM((1, width), F32),
            pltpu.VMEM(taps.shape, BF16),
            pltpu.VMEM((1, tokens), jnp.int32),
            pltpu.VMEM((1, width), F32),
            pltpu.VMEM(block, BF16),
            pltpu.VMEM((far,) + block, BF16),
            pltpu.VMEM((2, 16, width // 2), BF16),
            pltpu.VMEM((far + 1, 16, 2 * GW), BF16),
            pltpu.VMEM((far + 1,) + block, BF16),
            pltpu.VMEM((far + 1, tokens, GW), BF16),
            pltpu.VMEM(block, F32),
            pltpu.VMEM(block, F32),
            pltpu.VMEM((m, 1, tokens), F32),
            dma((8,)),
            dma((2,)),
            dma((far,)),
            dma((far,)),
            dma((far, groups)),
            dma((far, groups)),
            dma((groups,)),
            dma((m - 1,)),
            dma((m - 1,)),
        ],
        compiler_params=pltpu.CompilerParams(
            collective_id=0, has_side_effects=True, vmem_limit_bytes=40 * 1024 * 1024
        ),
        cost_estimate=pl.CostEstimate(
            flops=2 * tokens * tokens * width * (far + 1), bytes_accessed=8 * tokens * width, transcendentals=0
        ),
        name="mixer",
    )(*[
        pltpu.with_memory_space_constraint(x, pltpu.HBM)
        for x in (q_in, k_in, v_in, fir, skip[None, :], taps, segments[None, :], gain[None, :])
    ])


def solution(mesh):
    return jax.shard_map(
        functools.partial(on_device, mesh.shape["ctx"], mesh.shape["grp"]),
        mesh=mesh,
        in_specs=(
            P("ctx", "grp"),
            P("ctx", "grp"),
            P("ctx", "grp"),
            P(None, None, "grp"),
            P("grp"),
            P("grp", None),
            P("ctx"),
            P("grp"),
        ),
        out_specs=P("ctx", "grp"),
        check_vma=False,
    )
```

```python
import functools

import jax
import jax.numpy as jnp
from jax import lax
from jax.experimental import pallas as pl
from jax.experimental.pallas import tpu as pltpu
from jax.sharding import PartitionSpec as P

D = 8192
GW = 128
F32 = jnp.float32
BF16 = jnp.bfloat16
MESH = pl.DeviceIdType.MESH


def lagged(x, by, rows):
    return jnp.where(rows >= by, pltpu.roll(x, by, 0), 0.0)


def kernel(
    n, m, groups,
    q_hbm, k_hbm, v_hbm, fir_hbm, skip_hbm, taps_hbm, seg_hbm, gain_hbm, out,
    qbuf, kbuf, vbuf, fir, skip, taps, seg, gain, own, slots, halo, edges, mats, masks, acc, fq, sqs,
    in_sem, halo_sem, edge_send, edge_recv, kv_send, kv_recv, fwd_send, sq_send, sq_recv,
):
    me, gi = lax.axis_index("ctx"), lax.axis_index("grp")
    tokens, width = qbuf.shape
    far = n - 2
    relay = n == 4
    relayed = groups - max(1, groups // 4)

    pairs = (
        (k_hbm, kbuf), (v_hbm, vbuf), (q_hbm, qbuf), (fir_hbm, fir),
        (seg_hbm, seg), (taps_hbm, taps), (skip_hbm, skip), (gain_hbm, gain),
    )
    loads = [pltpu.make_async_copy(src, dst, in_sem.at[i]) for i, (src, dst) in enumerate(pairs)]
    for load in loads:
        load.start()
    barrier = pltpu.get_barrier_semaphore()
    for d in range(1, n):
        pl.semaphore_signal(barrier, inc=1, device_id={"ctx": lax.rem(me + d, n)}, device_id_type=MESH)
    for e in range(1, m):
        pl.semaphore_signal(barrier, inc=1, device_id={"grp": lax.rem(gi + e, m)}, device_id_type=MESH)
    def halo_copy(peer):
        return pltpu.make_async_remote_copy(
            src_ref=halo.at[0], dst_ref=halo.at[1], send_sem=halo_sem.at[0], recv_sem=halo_sem.at[1],
            device_id={"ctx": peer}, device_id_type=MESH)

    def edge_copy(d, peer):
        return pltpu.make_async_remote_copy(
            src_ref=edges.at[0], dst_ref=edges.at[d], send_sem=edge_send.at[d - 1], recv_sem=edge_recv.at[d - 1],
            device_id={"ctx": peer}, device_id_type=MESH)

    def kv_copy(d, g, peer):
        return pltpu.make_async_remote_copy(
            src_ref=own.at[g], dst_ref=slots.at[d - 1, g], send_sem=kv_send.at[d - 1, g],
            recv_sem=kv_recv.at[d - 1, g], device_id={"ctx": peer}, device_id_type=MESH)

    def forward(g):
        return pltpu.make_async_remote_copy(
            src_ref=slots.at[1, g], dst_ref=slots.at[0, g], send_sem=fwd_send.at[g],
            recv_sem=kv_recv.at[0, g], device_id={"ctx": 2}, device_id_type=MESH)

    def sends(d, g):
        there = me + d < n
        return there & (me != 1) if relay and d == 1 else there

    def pass_on(g):
        if relay and g < relayed:
            @pl.when(me == 3)
            def _():
                kv_copy(2, g, 1).wait_recv()
                forward(g).start()

    rows = lax.broadcasted_iota(jnp.int32, (tokens, GW), 0)
    cols = lax.broadcasted_iota(jnp.int32, (tokens, GW), 1)
    row8 = lax.broadcasted_iota(jnp.int32, (8, width), 0)
    for load in loads:
        load.wait()

    def last8(ref, by):
        return pltpu.roll(ref[tokens - 16 :, :].astype(F32)[8:], by, 0)

    def first8(ref, by):
        return pltpu.roll(ref[:16, :].astype(F32)[:8], by, 0)

    half = width // 2
    last = jnp.where(row8 < 2, last8(kbuf, 2), jnp.where(row8 < 4, last8(qbuf, 4), last8(vbuf, 6)))
    halo[0] = jnp.concatenate([last[:, :half], last[:, half:]], axis=0).astype(BF16)

    def product(g):
        lane = slice(g * GW, (g + 1) * GW)

        def filtered(ref, a):
            x = ref[:, lane].astype(F32)
            return (fir[a, 0:1, lane] * x + fir[a, 1:2, lane] * lagged(x, 1, rows)
                    + fir[a, 2:3, lane] * lagged(x, 2, rows))

        own[g] = (filtered(kbuf, 1) * filtered(vbuf, 2)).astype(BF16)

    def send_chunk(g):
        for d in range(far, 0, -1):
            @pl.when(sends(d, g) & (me != 0) if relay and d == 1 else sends(d, g))
            def _():
                kv_copy(d, g, me + d).start()
        if relay and g >= lag:
            late_chunk(g - lag)

    lag = min(2, groups)

    def late_chunk(g):
        @pl.when(me == 0)
        def _():
            kv_copy(1, g, 1).start()

    direct = range(relayed, groups) if relay else range(0)
    for g in (*direct, 0):
        product(g)
    pl.semaphore_wait(barrier, n - 1 + m - 1)
    @pl.when(me + 1 < n)
    def _():
        halo_copy(me + 1).start()

    if relay:
        @pl.when(me == 1)
        def _():
            for g in direct:
                kv_copy(1, g, 2).start()

    send_chunk(0)
    early = min(3, groups)
    for g in range(1, early):
        product(g)
        send_chunk(g)

    @pl.when(me >= 1)
    def _():
        halo_copy(me - 1).wait_recv()

    before = halo[1].astype(F32)
    before = jnp.where(me >= 1, jnp.concatenate([before[:8], before[8:]], axis=1), 0.0)
    edge = jnp.where(
        lax.rem(row8, 4) < 2, before, jnp.where(row8 < 4, first8(kbuf, 2), first8(vbuf, 6)))
    tap = [jnp.where(row8 < 4, fir[1, i : i + 1, :], fir[2, i : i + 1, :]) for i in range(3)]
    both = tap[0] * edge + tap[1] * pltpu.roll(edge, 1, 0) + tap[2] * pltpu.roll(edge, 2, 0)
    fix = pltpu.roll(both * pltpu.roll(both, 4, 0), 6, 0)
    small8 = row8[:, :GW]
    folded = [jnp.zeros((8, GW), F32)] * 2
    for g in range(groups):
        t, j = g // 4, 2 * (g % 4)
        piece = fix[:, g * GW : (g + 1) * GW]
        piece = pltpu.roll(piece, j, 0) if j else piece
        folded[t] = jnp.where((small8 >= j) & (small8 < j + 2), piece, folded[t])
    seg_f = seg[...].astype(F32)
    edges[0] = jnp.concatenate(
        [jnp.concatenate(folded, axis=0), jnp.broadcast_to(seg_f, (16, GW))], axis=1).astype(BF16)
    for d in range(1, far + 1):
        @pl.when(me + d < n)
        def _():
            edge_copy(d, me + d).start()
    passed = 0
    for g in range(early, groups):
        if g not in direct:
            product(g)
        send_chunk(g)
        if relay and g == groups - 1:
            for h in range(groups - lag, groups):
                late_chunk(h)
        if g >= early + 2:
            pass_on(passed)
            passed += 1

    def block_of(ref, d, g):
        t, j = g // 4, 2 * (g % 4)
        first = edges[d].astype(F32)[8 * t : 8 * t + 8, :GW]
        first = pltpu.roll(first, 8 - j, 0) if j else first
        whole = ref[...]
        top = whole[:16].astype(F32)
        head = jnp.concatenate([jnp.where(small8 < 2, first, top[:8]), top[8:]], axis=0)
        return jnp.concatenate([head.astype(BF16), whole[16:]], axis=0)

    flip = (rows + cols == GW - 1).astype(BF16)
    target = jnp.broadcast_to(seg_f, (tokens, GW)).T

    def mask(d):
        return jnp.where(edges[d].astype(F32)[:1, GW:] == target, 1.0, 0.0).astype(BF16)

    masks[0] = mask(0)
    back = [
        jnp.dot(taps[:, d * GW : (d + 1) * GW], flip, preferred_element_type=F32) for d in range(far + 1)
    ]
    for g in range(groups):
        lane = slice(g * GW, (g + 1) * GW)
        nearer = 0.0
        for d in range(far + 1):
            turned = pltpu.roll(jnp.broadcast_to(back[d][g : g + 1], (tokens, GW)), 1, 1, stride=1, stride_axis=0)
            mats[d, g] = jnp.where(cols <= rows, turned, nearer).astype(BF16)
            nearer = turned
        block = block_of(own.at[g], 0, g)
        acc[g] = (jnp.dot(mats[0, g] * masks[0], block, preferred_element_type=F32)
                  + skip[:, lane] * block.astype(F32))
        x = qbuf[:, lane].astype(F32)
        one = jnp.where(rows < 1, before[3:4, lane], pltpu.roll(x, 1, 0))
        two = jnp.where(rows < 1, before[2:3, lane], jnp.where(rows < 2, before[3:4, lane], pltpu.roll(x, 2, 0)))
        fq[g] = fir[0, 0:1, lane] * x + fir[0, 1:2, lane] * one + fir[0, 2:3, lane] * two
        if g % 3 == 1:
            pass_on(passed)
            passed += 1

    for d in range(1, far + 1):
        @pl.when(me >= d)
        def _():
            edge_copy(d, me - d).wait_recv()
            masks[d] = mask(d)

    def receive(d, g):
        if relay and d == 2 and g < relayed:
            @pl.when(me == 2)
            def _():
                kv_copy(d, g, me - d).wait_recv()
        else:
            kv_copy(d, g, me - d).wait_recv()

    def add_blocks(pair, sources):
        for g in pair:
            for d in sources:
                receive(d, g)
        for g in pair:
            left = jnp.concatenate([mats[d, g] * masks[d] for d in sources], axis=1)
            right = jnp.concatenate([block_of(slots.at[d - 1, g], d, g) for d in sources], axis=0)
            acc[g] += jnp.dot(left, right, preferred_element_type=F32)

    squares = jnp.zeros((tokens, GW), F32)
    for start in range(0, groups, 2):
        pair = range(start, min(start + 2, groups))
        for g in pair:
            pass_on(passed)
            passed += 1
        if relay:
            pl.when(me == 1)(functools.partial(add_blocks, pair, (1,)))
            pl.when(me >= 2)(functools.partial(add_blocks, pair, (2, 1)))
        else:
            for d in range(far, 0, -1):
                pl.when(me >= d)(functools.partial(add_blocks, pair, (d,)))
        for g in pair:
            gated = fq[g] * acc[g]
            acc[g] = gated
            squares += gated * gated

    sqs[0] = jnp.sum(squares.T, axis=0, keepdims=True)

    if m == 8:
        z, core = lax.div(gi, 2), lax.rem(gi, 2)
        chips = (3 - z, lax.rem(z + 2, 4), z + 1 - 2 * lax.rem(z, 2))
        peers = [2 * chip + c for chip in chips for c in (core, 1 - core)] + [2 * z + 1 - core]
        sources = peers
    else:
        peers = [lax.rem(gi + e, m) for e in range(1, m)]
        sources = [lax.rem(gi + m - e, m) for e in range(1, m)]

    def sq_copy(e, peer):
        return pltpu.make_async_remote_copy(
            src_ref=sqs.at[0], dst_ref=sqs.at[e], send_sem=sq_send.at[e - 1], recv_sem=sq_recv.at[e - 1],
            device_id={"grp": peer}, device_id_type=MESH)

    for e in range(1, m):
        sq_copy(e, peers[e - 1]).start()

    @pl.when(me + 1 < n)
    def _():
        halo_copy(me + 1).wait_send()

    for d in range(1, far + 1):
        @pl.when(me + d < n)
        def _():
            edge_copy(d, me + d).wait_send()
    for d in range(1, far + 1):
        for g in range(groups):
            @pl.when(sends(d, g))
            def _():
                kv_copy(d, g, me + d).wait_send()
    if relay:
        @pl.when(me == 1)
        def _():
            for g in direct:
                kv_copy(1, g, 2).wait_send()

        @pl.when(me == 3)
        def _():
            for g in range(relayed):
                forward(g).wait_send()

    for e in range(1, m):
        sq_copy(e, sources[e - 1]).wait_recv()
    total = sqs[0]
    for e in range(1, m):
        total += sqs[e]
    scale = lax.rsqrt(total / D + 1e-06)
    scale = jnp.broadcast_to(scale, (GW, tokens)).T
    for g in range(groups):
        lane = slice(g * GW, (g + 1) * GW)
        out[:, lane] = (acc[g] * scale * gain[:, lane]).astype(BF16)

    for e in range(1, m):
        sq_copy(e, peers[e - 1]).wait_send()


def on_device(n, m, q_in, k_in, v_in, fir, skip, taps, segments, gain):
    tokens, width = q_in.shape
    groups = width // GW
    far = n - 2
    vmem = pl.BlockSpec(memory_space=pltpu.VMEM)
    hbm = pl.BlockSpec(memory_space=pltpu.HBM)
    block = (groups, tokens, GW)
    dma = pltpu.SemaphoreType.DMA
    return pl.pallas_call(
        functools.partial(kernel, n, m, groups),
        out_shape=pltpu.VMEM((tokens, width), BF16),
        in_specs=[hbm] * 8,
        out_specs=vmem,
        scratch_shapes=[
            pltpu.VMEM((tokens, width), BF16),
            pltpu.VMEM((tokens, width), BF16),
            pltpu.VMEM((tokens, width), BF16),
            pltpu.VMEM(fir.shape, F32),
            pltpu.VMEM((1, width), F32),
            pltpu.VMEM(taps.shape, BF16),
            pltpu.VMEM((1, tokens), jnp.int32),
            pltpu.VMEM((1, width), F32),
            pltpu.VMEM(block, BF16),
            pltpu.VMEM((far,) + block, BF16),
            pltpu.VMEM((2, 16, width // 2), BF16),
            pltpu.VMEM((far + 1, 16, 2 * GW), BF16),
            pltpu.VMEM((far + 1,) + block, BF16),
            pltpu.VMEM((far + 1, tokens, GW), BF16),
            pltpu.VMEM(block, F32),
            pltpu.VMEM(block, F32),
            pltpu.VMEM((m, 1, tokens), F32),
            dma((8,)),
            dma((2,)),
            dma((far,)),
            dma((far,)),
            dma((far, groups)),
            dma((far, groups)),
            dma((groups,)),
            dma((m - 1,)),
            dma((m - 1,)),
        ],
        compiler_params=pltpu.CompilerParams(
            collective_id=0, has_side_effects=True, vmem_limit_bytes=40 * 1024 * 1024
        ),
        cost_estimate=pl.CostEstimate(
            flops=2 * tokens * tokens * width * (far + 1), bytes_accessed=8 * tokens * width, transcendentals=0
        ),
        name="mixer",
    )(*[
        pltpu.with_memory_space_constraint(x, pltpu.HBM)
        for x in (q_in, k_in, v_in, fir, skip[None, :], taps, segments[None, :], gain[None, :])
    ])


def solution(mesh):
    return jax.shard_map(
        functools.partial(on_device, mesh.shape["ctx"], mesh.shape["grp"]),
        mesh=mesh,
        in_specs=(
            P("ctx", "grp"),
            P("ctx", "grp"),
            P("ctx", "grp"),
            P(None, None, "grp"),
            P("grp"),
            P("grp", None),
            P("ctx"),
            P("grp"),
        ),
        out_specs=P("ctx", "grp"),
        check_vma=False,
    )
```

```python
import functools

import jax
import jax.numpy as jnp
from jax import lax
from jax.experimental import pallas as pl
from jax.experimental.pallas import tpu as pltpu
from jax.sharding import PartitionSpec as P

D = 8192
GW = 128
F32 = jnp.float32
BF16 = jnp.bfloat16
MESH = pl.DeviceIdType.MESH


def lagged(x, by, rows):
    return jnp.where(rows >= by, pltpu.roll(x, by, 0), 0.0)


def kernel(
    n, m, groups,
    q_hbm, k_hbm, v_hbm, fir_hbm, skip_hbm, taps_hbm, seg_hbm, gain_hbm, out,
    qbuf, kbuf, vbuf, fir, skip, taps, seg, gain, own, slots, halo, edges, mats, masks, acc, fq, sqs,
    in_sem, halo_sem, edge_send, edge_recv, kv_send, kv_recv, fwd_send, sq_send, sq_recv,
):
    me, gi = lax.axis_index("ctx"), lax.axis_index("grp")
    tokens, width = qbuf.shape
    far = n - 2
    relay = n == 4
    relayed = groups - max(1, groups // 8)

    pairs = (
        (k_hbm, kbuf), (v_hbm, vbuf), (q_hbm, qbuf), (fir_hbm, fir),
        (seg_hbm, seg), (taps_hbm, taps), (skip_hbm, skip), (gain_hbm, gain),
    )
    loads = [pltpu.make_async_copy(src, dst, in_sem.at[i]) for i, (src, dst) in enumerate(pairs)]
    for load in loads:
        load.start()
    barrier = pltpu.get_barrier_semaphore()
    for d in range(1, n):
        pl.semaphore_signal(barrier, inc=1, device_id={"ctx": lax.rem(me + d, n)}, device_id_type=MESH)
    for e in range(1, m):
        pl.semaphore_signal(barrier, inc=1, device_id={"grp": lax.rem(gi + e, m)}, device_id_type=MESH)
    def halo_copy(peer):
        return pltpu.make_async_remote_copy(
            src_ref=halo.at[0], dst_ref=halo.at[1], send_sem=halo_sem.at[0], recv_sem=halo_sem.at[1],
            device_id={"ctx": peer}, device_id_type=MESH)

    def edge_copy(d, peer):
        return pltpu.make_async_remote_copy(
            src_ref=edges.at[0], dst_ref=edges.at[d], send_sem=edge_send.at[d - 1], recv_sem=edge_recv.at[d - 1],
            device_id={"ctx": peer}, device_id_type=MESH)

    def kv_copy(d, g, peer):
        return pltpu.make_async_remote_copy(
            src_ref=own.at[g], dst_ref=slots.at[d - 1, g], send_sem=kv_send.at[d - 1, g],
            recv_sem=kv_recv.at[d - 1, g], device_id={"ctx": peer}, device_id_type=MESH)

    def forward(g):
        return pltpu.make_async_remote_copy(
            src_ref=slots.at[1, g], dst_ref=slots.at[0, g], send_sem=fwd_send.at[g],
            recv_sem=kv_recv.at[0, g], device_id={"ctx": 2}, device_id_type=MESH)

    def sends(d, g):
        there = me + d < n
        return there & (me != 1) if relay and d == 1 else there

    def pass_on(g):
        if relay and g < relayed:
            @pl.when(me == 3)
            def _():
                kv_copy(2, g, 1).wait_recv()
                forward(g).start()

    rows = lax.broadcasted_iota(jnp.int32, (tokens, GW), 0)
    cols = lax.broadcasted_iota(jnp.int32, (tokens, GW), 1)
    row8 = lax.broadcasted_iota(jnp.int32, (8, width), 0)
    for load in loads:
        load.wait()

    def last8(ref, by):
        return pltpu.roll(ref[tokens - 16 :, :].astype(F32)[8:], by, 0)

    def first8(ref, by):
        return pltpu.roll(ref[:16, :].astype(F32)[:8], by, 0)

    half = width // 2
    last = jnp.where(row8 < 2, last8(kbuf, 2), jnp.where(row8 < 4, last8(qbuf, 4), last8(vbuf, 6)))
    halo[0] = jnp.concatenate([last[:, :half], last[:, half:]], axis=0).astype(BF16)

    def product(g):
        lane = slice(g * GW, (g + 1) * GW)

        def filtered(ref, a):
            x = ref[:, lane].astype(F32)
            return (fir[a, 0:1, lane] * x + fir[a, 1:2, lane] * lagged(x, 1, rows)
                    + fir[a, 2:3, lane] * lagged(x, 2, rows))

        own[g] = (filtered(kbuf, 1) * filtered(vbuf, 2)).astype(BF16)

    def send_chunk(g):
        for d in range(far, 0, -1):
            @pl.when(sends(d, g))
            def _():
                kv_copy(d, g, me + d).start()

    direct = range(relayed, groups) if relay else range(0)
    for g in (*direct, 0):
        product(g)
    pl.semaphore_wait(barrier, n - 1 + m - 1)
    @pl.when(me + 1 < n)
    def _():
        halo_copy(me + 1).start()

    if relay:
        @pl.when(me == 1)
        def _():
            for g in direct:
                kv_copy(1, g, 2).start()

    send_chunk(0)
    early = min(3, groups)
    for g in range(1, early):
        product(g)
        send_chunk(g)

    @pl.when(me >= 1)
    def _():
        halo_copy(me - 1).wait_recv()

    before = halo[1].astype(F32)
    before = jnp.where(me >= 1, jnp.concatenate([before[:8], before[8:]], axis=1), 0.0)
    edge = jnp.where(
        lax.rem(row8, 4) < 2, before, jnp.where(row8 < 4, first8(kbuf, 2), first8(vbuf, 6)))
    tap = [jnp.where(row8 < 4, fir[1, i : i + 1, :], fir[2, i : i + 1, :]) for i in range(3)]
    both = tap[0] * edge + tap[1] * pltpu.roll(edge, 1, 0) + tap[2] * pltpu.roll(edge, 2, 0)
    fix = pltpu.roll(both * pltpu.roll(both, 4, 0), 6, 0)
    small8 = row8[:, :GW]
    folded = [jnp.zeros((8, GW), F32)] * 2
    for g in range(groups):
        t, j = g // 4, 2 * (g % 4)
        piece = fix[:, g * GW : (g + 1) * GW]
        piece = pltpu.roll(piece, j, 0) if j else piece
        folded[t] = jnp.where((small8 >= j) & (small8 < j + 2), piece, folded[t])
    seg_f = seg[...].astype(F32)
    edges[0] = jnp.concatenate(
        [jnp.concatenate(folded, axis=0), jnp.broadcast_to(seg_f, (16, GW))], axis=1).astype(BF16)
    for d in range(1, far + 1):
        @pl.when(me + d < n)
        def _():
            edge_copy(d, me + d).start()
    passed = 0
    for g in range(early, groups):
        if g not in direct:
            product(g)
        send_chunk(g)
        if g >= early + 2:
            pass_on(passed)
            passed += 1

    def block_of(ref, d, g):
        t, j = g // 4, 2 * (g % 4)
        first = edges[d].astype(F32)[8 * t : 8 * t + 8, :GW]
        first = pltpu.roll(first, 8 - j, 0) if j else first
        whole = ref[...]
        top = whole[:16].astype(F32)
        head = jnp.concatenate([jnp.where(small8 < 2, first, top[:8]), top[8:]], axis=0)
        return jnp.concatenate([head.astype(BF16), whole[16:]], axis=0)

    flip = (rows + cols == GW - 1).astype(BF16)
    target = jnp.broadcast_to(seg_f, (tokens, GW)).T

    def mask(d):
        return jnp.where(edges[d].astype(F32)[:1, GW:] == target, 1.0, 0.0).astype(BF16)

    masks[0] = mask(0)
    back = [
        jnp.dot(taps[:, d * GW : (d + 1) * GW], flip, preferred_element_type=F32) for d in range(far + 1)
    ]
    for g in range(groups):
        lane = slice(g * GW, (g + 1) * GW)
        nearer = 0.0
        for d in range(far + 1):
            turned = pltpu.roll(jnp.broadcast_to(back[d][g : g + 1], (tokens, GW)), 1, 1, stride=1, stride_axis=0)
            mats[d, g] = jnp.where(cols <= rows, turned, nearer).astype(BF16)
            nearer = turned
        block = block_of(own.at[g], 0, g)
        acc[g] = (jnp.dot(mats[0, g] * masks[0], block, preferred_element_type=F32)
                  + skip[:, lane] * block.astype(F32))
        x = qbuf[:, lane].astype(F32)
        one = jnp.where(rows < 1, before[3:4, lane], pltpu.roll(x, 1, 0))
        two = jnp.where(rows < 1, before[2:3, lane], jnp.where(rows < 2, before[3:4, lane], pltpu.roll(x, 2, 0)))
        fq[g] = fir[0, 0:1, lane] * x + fir[0, 1:2, lane] * one + fir[0, 2:3, lane] * two
        if g % 2 == 1:
            pass_on(passed)
            passed += 1

    for d in range(1, far + 1):
        @pl.when(me >= d)
        def _():
            edge_copy(d, me - d).wait_recv()
            masks[d] = mask(d)

    def receive(d, g):
        if relay and d == 2 and g < relayed:
            @pl.when(me == 2)
            def _():
                kv_copy(d, g, me - d).wait_recv()
        else:
            kv_copy(d, g, me - d).wait_recv()

    def add_blocks(pair, sources):
        for g in pair:
            for d in sources:
                receive(d, g)
        for g in pair:
            left = jnp.concatenate([mats[d, g] * masks[d] for d in sources], axis=1)
            right = jnp.concatenate([block_of(slots.at[d - 1, g], d, g) for d in sources], axis=0)
            acc[g] += jnp.dot(left, right, preferred_element_type=F32)

    squares = jnp.zeros((tokens, GW), F32)
    for start in range(0, groups, 2):
        pair = range(start, min(start + 2, groups))
        for g in pair:
            pass_on(passed)
            passed += 1
        if relay:
            pl.when(me == 1)(functools.partial(add_blocks, pair, (1,)))
            pl.when(me >= 2)(functools.partial(add_blocks, pair, (2, 1)))
        else:
            for d in range(far, 0, -1):
                pl.when(me >= d)(functools.partial(add_blocks, pair, (d,)))
        for g in pair:
            gated = fq[g] * acc[g]
            acc[g] = gated
            squares += gated * gated

    sqs[0] = jnp.sum(squares.T, axis=0, keepdims=True)

    if m == 8:
        z, core = lax.div(gi, 2), lax.rem(gi, 2)
        chips = (3 - z, lax.rem(z + 2, 4), z + 1 - 2 * lax.rem(z, 2))
        peers = [2 * chip + c for chip in chips for c in (core, 1 - core)] + [2 * z + 1 - core]
        sources = peers
    else:
        peers = [lax.rem(gi + e, m) for e in range(1, m)]
        sources = [lax.rem(gi + m - e, m) for e in range(1, m)]

    def sq_copy(e, peer):
        return pltpu.make_async_remote_copy(
            src_ref=sqs.at[0], dst_ref=sqs.at[e], send_sem=sq_send.at[e - 1], recv_sem=sq_recv.at[e - 1],
            device_id={"grp": peer}, device_id_type=MESH)

    for e in range(1, m):
        sq_copy(e, peers[e - 1]).start()

    @pl.when(me + 1 < n)
    def _():
        halo_copy(me + 1).wait_send()

    for d in range(1, far + 1):
        @pl.when(me + d < n)
        def _():
            edge_copy(d, me + d).wait_send()
    for d in range(1, far + 1):
        for g in range(groups):
            @pl.when(sends(d, g))
            def _():
                kv_copy(d, g, me + d).wait_send()
    if relay:
        @pl.when(me == 1)
        def _():
            for g in direct:
                kv_copy(1, g, 2).wait_send()

        @pl.when(me == 3)
        def _():
            for g in range(relayed):
                forward(g).wait_send()

    for e in range(1, m):
        sq_copy(e, sources[e - 1]).wait_recv()
    total = sqs[0]
    for e in range(1, m):
        total += sqs[e]
    scale = lax.rsqrt(total / D + 1e-06)
    scale = jnp.broadcast_to(scale, (GW, tokens)).T
    for g in range(groups):
        lane = slice(g * GW, (g + 1) * GW)
        out[:, lane] = (acc[g] * scale * gain[:, lane]).astype(BF16)

    for e in range(1, m):
        sq_copy(e, peers[e - 1]).wait_send()


def on_device(n, m, q_in, k_in, v_in, fir, skip, taps, segments, gain):
    tokens, width = q_in.shape
    groups = width // GW
    far = n - 2
    vmem = pl.BlockSpec(memory_space=pltpu.VMEM)
    hbm = pl.BlockSpec(memory_space=pltpu.HBM)
    block = (groups, tokens, GW)
    dma = pltpu.SemaphoreType.DMA
    return pl.pallas_call(
        functools.partial(kernel, n, m, groups),
        out_shape=pltpu.VMEM((tokens, width), BF16),
        in_specs=[hbm] * 8,
        out_specs=vmem,
        scratch_shapes=[
            pltpu.VMEM((tokens, width), BF16),
            pltpu.VMEM((tokens, width), BF16),
            pltpu.VMEM((tokens, width), BF16),
            pltpu.VMEM(fir.shape, F32),
            pltpu.VMEM((1, width), F32),
            pltpu.VMEM(taps.shape, BF16),
            pltpu.VMEM((1, tokens), jnp.int32),
            pltpu.VMEM((1, width), F32),
            pltpu.VMEM(block, BF16),
            pltpu.VMEM((far,) + block, BF16),
            pltpu.VMEM((2, 16, width // 2), BF16),
            pltpu.VMEM((far + 1, 16, 2 * GW), BF16),
            pltpu.VMEM((far + 1,) + block, BF16),
            pltpu.VMEM((far + 1, tokens, GW), BF16),
            pltpu.VMEM(block, F32),
            pltpu.VMEM(block, F32),
            pltpu.VMEM((m, 1, tokens), F32),
            dma((8,)),
            dma((2,)),
            dma((far,)),
            dma((far,)),
            dma((far, groups)),
            dma((far, groups)),
            dma((groups,)),
            dma((m - 1,)),
            dma((m - 1,)),
        ],
        compiler_params=pltpu.CompilerParams(
            collective_id=0, has_side_effects=True, vmem_limit_bytes=40 * 1024 * 1024
        ),
        cost_estimate=pl.CostEstimate(
            flops=2 * tokens * tokens * width * (far + 1), bytes_accessed=8 * tokens * width, transcendentals=0
        ),
        name="mixer",
    )(*[
        pltpu.with_memory_space_constraint(x, pltpu.HBM)
        for x in (q_in, k_in, v_in, fir, skip[None, :], taps, segments[None, :], gain[None, :])
    ])


def solution(mesh):
    return jax.shard_map(
        functools.partial(on_device, mesh.shape["ctx"], mesh.shape["grp"]),
        mesh=mesh,
        in_specs=(
            P("ctx", "grp"),
            P("ctx", "grp"),
            P("ctx", "grp"),
            P(None, None, "grp"),
            P("grp"),
            P("grp", None),
            P("ctx"),
            P("grp"),
        ),
        out_specs=P("ctx", "grp"),
        check_vma=False,
    )
```
